128 devices in a mesh: slab: 32 (over x, z, core), cable: 4 (over y).
Axes of the slice: x: 4, y: 4, z: 4, core: 2. Of those that a mesh axis runs over, the one named last changes fastest.
Arguments:
- electric: float32 [3, 1024, 128, 256], P(None, ('slab', 'cable')), may hold values from -6 to 6
- magnetic: float32 [3, 1024, 128, 256], P(None, ('slab', 'cable')), may hold values from -6 to 6
- conductivity: float32 [1024, 128, 256], P(('slab', 'cable')), may hold values from 0.02 to 0.8
- voltage: float32 [32, 128, 16384], P(None, None, ('slab', 'cable')), may hold values from -6 to 6
- current: float32 [32, 128, 16384], P(None, None, ('slab', 'cable')), may hold values from -6 to 6
- inverse_inductance: float32 [32, 32, 16384], P(None, None, ('slab', 'cable')), as said below
- inverse_capacitance: float32 [32, 32, 16384], P(None, None, ('slab', 'cable')), as said below
- tangent: float32 [3, 128, 16384], P(None, ('slab', 'cable')), may hold values from -4 to 4
- sample_cell: int32 [128, 16384], P(('slab', 'cable')), may hold values from 0 to 1023
- tube_length: int32 [16384], P(('slab', 'cable')), may hold values from 32 to 128
- junction_link: int32 [16384], P(('slab', 'cable')), may hold values from 0 to 127, as said below
Outputs:
- electric_new: float32 [3, 1024, 128, 256], P(None, ('slab', 'cable'))
- magnetic_new: float32 [3, 1024, 128, 256], P(None, ('slab', 'cable'))
- voltage_new: float32 [32, 128, 16384], P(None, None, ('slab', 'cable'))
- current_new: float32 [32, 128, 16384], P(None, None, ('slab', 'cable'))
The draws below stay inside these ranges and needn't reach their ends.
Inputs may be any that keep to these rules, and one draw needn't show every extreme that they name: `junction_link`: every aligned block of 128 entries holds each of its values once. `inverse_inductance`: symmetric, with off-diagonal entries summing to about as much as the diagonal. `inverse_capacitance`: symmetric, with off-diagonal entries summing to about as much as the diagonal.
All inputs are finite; a program needn't handle non-finite values.
Results may differ from the reference program's by a relative error of at most 0.0001.
Values sent between devices are 32-bit elements; how exact they have to be, the bound alone decides.
No kernel may reach another device: no remote copies, remote signals or barrier semaphores. Data moves between devices by JAX's collectives and lax.ppermute only.
A program may use at most 128 MiB of HBM per device.

```python
import math
import jax
import jax.numpy as jnp
from jax import lax

COND = 32
SUB = 3
SEG_DEV = 1
CX = 8
NY = 128
NZ = 256
TUBE_DEV = 128
NX = 1024
SEG = 128
TUBES = 16384
N_CABLE = 4


def matrix_block(subkey):
    first, second = jax.random.split(subkey)
    diagonal = jax.random.uniform(first, (COND, TUBES), jnp.float32, 0.3, 0.6)
    spread = 0.025
    coupling = jax.random.normal(second, (COND, COND, TUBES), jnp.float32) * spread
    coupling = 0.5 * (coupling + jnp.transpose(coupling, (1, 0, 2)))
    identity = jnp.eye(COND, dtype=jnp.float32)[:, :, None]
    return coupling * (1.0 - identity) + identity * diagonal[None]


def draw_inverse_inductance(key, part):
    return matrix_block(jax.random.fold_in(key, 11))


def draw_inverse_capacitance(key, part):
    return matrix_block(jax.random.fold_in(key, 23))


def draw_tube_length(key, part):
    values = jax.random.randint(jax.random.fold_in(key, 5), (TUBES,), SEG // 4, SEG + 1).astype(jnp.int32)
    return values.at[0].set(SEG).at[1].set(SEG // 4)


def one_block(subkey):
    return jax.random.permutation(subkey, TUBE_DEV)


def draw_junction_link(key, part):
    subkeys = jax.random.split(jax.random.fold_in(key, 7), TUBES // TUBE_DEV)
    return jax.vmap(one_block)(subkeys).reshape(TUBES).astype(jnp.int32)


def with_ends(values, own_key, smallest, largest):
    longest = values.shape.index(max(values.shape))
    spots = []
    for shift in (0, 1):
        where = [jax.random.randint(jax.random.fold_in(own_key, axis), (), 0, length) for axis, length in enumerate(values.shape)]
        where[longest] = (where[longest] + shift) % values.shape[longest]
        spots.append(tuple(where))
    return values.at[spots[0]].set(smallest).at[spots[1]].set(largest)


def steps_of(rng, dims, cuts, low, top_value):
    def one(dim, shards_of):
        heights = jax.random.uniform(jax.random.fold_in(jax.random.fold_in(rng, 6), dim), (shards_of,), jnp.float32, low / len(cuts), top_value / len(cuts))
        return jnp.repeat(jnp.exp(heights), dims[dim] // shards_of).reshape((-1,) + (1,) * (len(dims) - dim - 1))

    level = one(*cuts[0])
    for cut in cuts[1:]:
        level = level * one(*cut)
    return level


def scatter_about(own_key, shape, deviation, most, pieces=(), held_as=jnp.bfloat16):
    array = jax.random.normal(own_key, shape, jnp.float32) * deviation
    if len(pieces) > 0:
        array = steps_of(own_key, shape, pieces, -0.22, 0.18) * array
    return jnp.clip(array, min=-most, max=most).astype(held_as)


def setup_inputs(seed: int = 0) -> dict:
    key_list = jax.random.split(jax.random.key(seed), 12)
    return {
        "electric": scatter_about(key_list[0], (3, NX, NY, NZ), 1.0, 6.0, ((1, 128),), jnp.float32),
        "magnetic": scatter_about(key_list[1], (3, NX, NY, NZ), 1.0, 6.0, ((1, 128),), jnp.float32),
        "conductivity": jnp.clip(jnp.exp(math.log(0.8) - 3.6888795 * jax.random.uniform(key_list[2], (NX, NY, NZ), jnp.float32) ** steps_of(key_list[2], (NX, NY, NZ), ((0, 128),), -0.2, 0.2)), 0.02, 0.8),
        "voltage": scatter_about(key_list[3], (COND, SEG, TUBES), 1.0, 6.0, ((2, 128),), jnp.float32),
        "current": scatter_about(key_list[4], (COND, SEG, TUBES), 1.0, 6.0, ((2, 128),), jnp.float32),
        "inverse_inductance": draw_inverse_inductance(jax.random.fold_in(key_list[11], 71), 0),
        "inverse_capacitance": draw_inverse_capacitance(jax.random.fold_in(key_list[11], 71), 0),
        "tangent": scatter_about(key_list[7], (3, SEG, TUBES), 1.0, 4.0, ((1, 128),), jnp.float32),
        "sample_cell": with_ends(jax.random.randint(key_list[8], (SEG, TUBES), 0, CX * NY), jax.random.fold_in(key_list[8], 1), 0, (CX * NY) - 1).astype(jnp.int32),
        "tube_length": draw_tube_length(jax.random.fold_in(key_list[11], 71), 0),
        "junction_link": draw_junction_link(jax.random.fold_in(key_list[11], 71), 0),
    }


courant = 0.5
highest = lax.Precision.HIGHEST


def forward_diff(quantity, along):
    extent = quantity.shape[along]
    shifted = jnp.concatenate([lax.slice_in_dim(quantity, 1, extent, axis=along), jnp.zeros_like(lax.slice_in_dim(quantity, 0, 1, axis=along))], axis=along)
    return shifted - quantity


def backward_diff(quantity, along):
    extent = quantity.shape[along]
    shifted = jnp.concatenate([jnp.zeros_like(lax.slice_in_dim(quantity, 0, 1, axis=along)), lax.slice_in_dim(quantity, 0, extent - 1, axis=along)], axis=along)
    return quantity - shifted


def reference(electric, magnetic, conductivity, voltage, current, inverse_inductance, inverse_capacitance, tangent, sample_cell, tube_length, junction_link):
    keep_factor = (1.0 - conductivity) / (1.0 + conductivity)
    curl_factor = courant / (1.0 + conductivity)
    magnetic_new = magnetic - courant * jnp.stack([
        forward_diff(electric[2], 1) - forward_diff(electric[1], 2),
        forward_diff(electric[0], 2) - forward_diff(electric[2], 0),
        forward_diff(electric[1], 0) - forward_diff(electric[0], 1)])
    segment_ids = jnp.arange(SEG, dtype=jnp.int32)
    tube_ids = jnp.arange(TUBES, dtype=jnp.int32)
    global_cell = (((segment_ids // SEG_DEV) * (CX * NY * NZ)).astype(jnp.int32)[:, None] + sample_cell * NZ + (tube_ids % NZ)[None, :]).astype(jnp.int32)
    flat_field = electric.reshape(3, -1)
    drive_field = tangent[0] * flat_field[0][global_cell] + tangent[1] * flat_field[1][global_cell] + tangent[2] * flat_field[2][global_cell]
    live = (segment_ids[:, None] < tube_length[None, :]).astype(jnp.float32)
    last_pick = (segment_ids[:, None] == (tube_length - 1)[None, :]).astype(jnp.float32)
    owner = jnp.arange(TUBES, dtype=jnp.int32) // TUBE_DEV
    feeder_owner = owner // N_CABLE * N_CABLE + (owner % N_CABLE + N_CABLE - 1) % N_CABLE
    feeder_tube = (feeder_owner * TUBE_DEV + junction_link).astype(jnp.int32)
    volts = voltage
    amps = current
    for substep in range(SUB):
        volts_next = jnp.concatenate([volts[:, 1:], jnp.zeros_like(volts[:, :1])], axis=1)
        push = volts_next - volts - drive_field[None]
        amps = live[None] * (amps - jnp.einsum('cdt,dst->cst', inverse_inductance, push, precision=highest))
        tube_end = jnp.sum(amps * last_pick[None], axis=1)
        inflow = tube_end[:, feeder_tube]
        amps_prev = jnp.concatenate([inflow[:, None], amps[:, :-1]], axis=1)
        volts = live[None] * (volts - jnp.einsum('cdt,dst->cst', inverse_capacitance, amps - amps_prev, precision=highest))
    induced = jnp.mean(amps, axis=0)
    flat_index = global_cell.reshape(-1)
    deposit = jnp.stack([jax.ops.segment_sum((tangent[component] * induced).reshape(-1), flat_index, num_segments=NX * NY * NZ) for component in range(3)]).reshape(electric.shape)
    curl_h = jnp.stack([
        backward_diff(magnetic_new[2], 1) - backward_diff(magnetic_new[1], 2),
        backward_diff(magnetic_new[0], 2) - backward_diff(magnetic_new[2], 0),
        backward_diff(magnetic_new[1], 0) - backward_diff(magnetic_new[0], 1)])
    electric_new = keep_factor[None] * electric + curl_factor[None] * (curl_h - deposit)
    return electric_new, magnetic_new, volts, amps
```

```python
import jax
import jax.numpy as jnp
from jax import lax
from jax.experimental import pallas as pl
from jax.experimental.pallas import tpu as pltpu
from jax.sharding import PartitionSpec as P

F = jnp.float32
B16 = jnp.bfloat16
I32 = jnp.int32
SUB = 3
COURANT = 0.5
MB = 2**20


def take(x, index, axis):
    return jnp.take_along_axis(x, index, axis=axis, mode="promise_in_bounds")


def iota(shape, axis):
    return lax.broadcasted_iota(I32, shape, axis)


def call(body, out, *ins, name, scratch=(), limit=40, in_specs=None, aliases=None, out_specs=None, cost=None, grid=()):
    kw = {}
    if in_specs is not None:
        kw["in_specs"] = in_specs
    if out_specs is not None:
        kw["out_specs"] = out_specs
    return pl.pallas_call(
        body,
        out_shape=out,
        grid=grid,
        scratch_shapes=list(scratch),
        input_output_aliases=aliases or {},
        compiler_params=pltpu.CompilerParams(vmem_limit_bytes=limit * MB),
        cost_estimate=cost,
        name=name,
        **kw,
    )(*ins)


def shape(*dims, dtype=F):
    return jax.ShapeDtypeStruct(dims, dtype)


def gather_kernel(e_ref, idx_ref, tan_ref, drive_ref, layer_ref):
    layer_ref[...] = e_ref[1:3, 0]
    for h in range(2):
        lanes = pl.ds(h * 128, 128)
        rows = pl.ds(h, 64, stride=2)
        idx = idx_ref[rows, :]
        idx = [idx[8 * g : 8 * g + 8] for g in range(8)]
        low = [i & 7 for i in idx]
        high = [i >> 3 for i in idx]

        def step(b, acc):
            acc = list(acc)
            x = b // 16
            yrows = pl.ds(pl.multiple_of((b % 16) * 8, 8), 8)
            src = [e_ref[k, x, yrows, lanes] for k in range(3)]
            for g in range(8):
                hit = high[g] == b
                for k in range(3):
                    acc[g * 3 + k] = jnp.where(hit, take(src[k], low[g], 0), acc[g * 3 + k])
            return tuple(acc)

        acc = lax.fori_loop(0, 128, step, (jnp.zeros((8, 128), F),) * 24, unroll=4)
        picked = [jnp.concatenate([acc[g * 3 + k] for g in range(8)], 0) for k in range(3)]
        steer = [tan_ref[k, rows, :] for k in range(3)]
        drive_ref[rows, :] = steer[0] * picked[0] + steer[1] * picked[1] + steer[2] * picked[2]


def merge_pair(x, y):
    low = iota((8, 128), 0) < 4
    return jnp.where(low, x, pltpu.roll(y, 4, 0)), jnp.where(low, pltpu.roll(x, 4, 0), y)


def split_parts(x):
    high = x.astype(B16)
    return high, (x - high.astype(F)).astype(B16)


def line_kernel(
    v_ref, i_ref, a_ref, b_ref, drive_ref, len_ref,
    vo_ref, io_ref, ends_ref, ind_ref,
    vt, it, at, vg, ig, ah, bh, dg, eg, indt,
):
    sub8 = iota((8, 128), 0)
    lane8 = iota((8, 128), 1)
    lane = iota((128, 128), 1)

    def turn_in(c, carry):
        vt[c] = v_ref[c].T
        it[c] = i_ref[c].T
        return carry

    lax.fori_loop(0, 32, turn_in, 0, unroll=4)

    spread = [(sub8 >> 2) + 2 * j for j in range(4)]
    own = (sub8 & 3) == (lane8 & 3)
    for m_ref, dst in ((a_ref, ah), (b_ref, bh)):

        def expand(c, carry):
            tiles = []
            for q in range(4):
                tile = m_ref[c, 8 * q : 8 * q + 8, :]
                for j in range(4):
                    tiles.append(jnp.where(own, take(tile, spread[j], 0), 0.0))
            at[c] = jnp.concatenate(tiles, 0).T
            return carry

        lax.fori_loop(0, 32, expand, 0, unroll=4)

        def pack(b, carry):
            rows = pl.ds(pl.multiple_of(b * 8, 8), 8)
            first, second = [], []
            for i in range(16):
                g0, g1 = merge_pair(at[2 * i, rows, :], at[2 * i + 1, rows, :])
                first.append(g0)
                second.append(g1)
            for p, tiles in enumerate((first, second)):
                high, low = split_parts(jnp.concatenate(tiles, 0))
                out_rows = pl.ds(pl.multiple_of(b * 256 + p * 128, 128), 128)
                dst[out_rows, 0:128] = high
                dst[out_rows, 128:256] = low
            return carry

        lax.fori_loop(0, 16, pack, 0, unroll=2)

    drive_t = drive_ref[...].T
    at[0] = drive_t
    at[1] = jnp.broadcast_to(len_ref[...].astype(F), (128, 128)).T
    for b in range(16):
        rows = slice(8 * b, 8 * b + 8)
        for p, value in enumerate(merge_pair(at[0, rows, :], at[0, rows, :])):
            dg[16 * b + 8 * p : 16 * b + 8 * p + 8, :] = value
        for p, value in enumerate(merge_pair(at[1, rows, :], at[1, rows, :])):
            eg[16 * b + 8 * p : 16 * b + 8 * p + 8, :] = value.astype(I32)

    def regroup(b, carry):
        rows = pl.ds(pl.multiple_of(b * 8, 8), 8)
        for src, dst in ((vt, vg), (it, ig)):
            for i in range(16):
                g0, g1 = merge_pair(src[2 * i, rows, :], src[2 * i + 1, rows, :])
                dst[pl.ds(pl.multiple_of(b * 256 + 8 * i, 8), 8), :] = g0
                dst[pl.ds(pl.multiple_of(b * 256 + 128 + 8 * i, 8), 8), :] = g1
        return carry

    lax.fori_loop(0, 16, regroup, 0, unroll=2)

    def product(m_ref, rows, x):
        high, low = split_parts(x)
        rhs = jnp.concatenate([high, low], 1)
        rhs = jnp.concatenate([rhs, rhs], 0)
        y = jnp.dot(m_ref[rows, :], rhs, preferred_element_type=F)
        return y[:, :128] + y[:, 128:]

    unroll = 16
    for substep in range(SUB):

        def current_step(n, acc):
            for u in range(unroll):
                g = n * unroll + u
                rows = pl.ds(pl.multiple_of(g * 128, 128), 128)
                small = pl.ds(pl.multiple_of(g * 8, 8), 8)
                length = eg[small, :]
                live = jnp.concatenate([lane8 < length] * 16, 0)
                drive = jnp.concatenate([dg[small, :]] * 16, 0)
                volts = vg[rows, :]
                ahead = jnp.where(lane == 127, 0.0, pltpu.roll(volts, 127, 1))
                y = product(ah, rows, ahead - volts - drive)
                amps = jnp.where(live, ig[rows, :] - y, 0.0)
                ig[rows, :] = amps
                spot = lane8 == 4 * g + (sub8 & 3)
                acc = tuple(
                    jnp.where(spot, take(amps[8 * i : 8 * i + 8], length - 1, 1), acc[i])
                    for i in range(16)
                )
            return acc

        acc = lax.fori_loop(0, 32 // unroll, current_step, (jnp.zeros((8, 128), F),) * 16)
        pick = (sub8 & 1) * 4 + (lane8 & 3)
        for q in range(4):
            out = take(acc[4 * q], pick, 0)
            for i in range(1, 4):
                out = jnp.where((sub8 >> 1) == i, take(acc[4 * q + i], pick, 0), out)
            ends_ref[substep, 8 * q : 8 * q + 8, :] = out

        def voltage_step(n, carry):
            for u in range(unroll):
                g = n * unroll + u
                rows = pl.ds(pl.multiple_of(g * 128, 128), 128)
                small = pl.ds(pl.multiple_of(g * 8, 8), 8)
                live = jnp.concatenate([lane8 < eg[small, :]] * 16, 0)
                amps = ig[rows, :]
                behind = jnp.where(lane == 0, 0.0, pltpu.roll(amps, 1, 1))
                y = product(bh, rows, amps - behind)
                vg[rows, :] = jnp.where(live, vg[rows, :] - y, 0.0)
            return carry

        lax.fori_loop(0, 32 // unroll, voltage_step, 0)

    def ungroup(b, carry):
        rows = pl.ds(pl.multiple_of(b * 8, 8), 8)
        for src, dst in ((vg, vt), (ig, it)):
            sums = [None, None]
            for i in range(16):
                g0 = src[pl.ds(pl.multiple_of(b * 256 + 8 * i, 8), 8), :]
                g1 = src[pl.ds(pl.multiple_of(b * 256 + 128 + 8 * i, 8), 8), :]
                c0, c1 = merge_pair(g0, g1)
                dst[2 * i, rows, :] = c0
                dst[2 * i + 1, rows, :] = c1
                if src is ig:
                    sums = [c0 + c1 if s is None else s + c0 + c1 for s in sums[:1]] + [None]
            if src is ig:
                indt[rows, :] = sums[0] * (1.0 / 32.0)
        return carry

    lax.fori_loop(0, 16, ungroup, 0, unroll=2)

    def turn_out(c, carry):
        vo_ref[c] = vt[c].T
        io_ref[c] = it[c].T
        return carry

    lax.fori_loop(0, 32, turn_out, 0, unroll=4)
    ind_ref[...] = indt[...].T


def lines(voltage, current, inductance, capacitance, drive, lengths):
    big = pltpu.VMEM((32, 128, 128), F)
    flat = pltpu.VMEM((4096, 128), F)
    packed = pltpu.VMEM((4096, 256), B16)
    return call(
        line_kernel,
        (shape(32, 128, 128), shape(32, 128, 128), shape(3, 32, 128), shape(128, 128)),
        voltage, current, inductance, capacitance, drive, lengths,
        name="lines",
        scratch=[big, big, big, flat, flat, packed, packed,
                 pltpu.VMEM((256, 128), F), pltpu.VMEM((256, 128), I32), pltpu.VMEM((128, 128), F)],
        limit=40,
    )


def junction_kernel(ends_ref, link_ref, a_ref, b_ref, v_ref, i_ref, ind_ref, vo_ref, io_ref, indo_ref, buf):
    link = jnp.broadcast_to(link_ref[...], (8, 128))
    inflow = [
        jnp.concatenate([take(ends_ref[k, 8 * q : 8 * q + 8, :], link, 1) for q in range(4)], 0)
        for k in range(SUB)
    ]

    def apply(m_ref, x):
        buf[...] = x
        parts = [None] * 4
        for d in range(32):
            term = m_ref[d] * buf[d : d + 1, :]
            parts[d % 4] = term if parts[d % 4] is None else parts[d % 4] + term
        return (parts[0] + parts[1]) + (parts[2] + parts[3])

    f1, f2, f3 = inflow
    v1 = apply(b_ref, f1)
    i2 = apply(a_ref, v1)
    v2b = apply(b_ref, i2)
    v2a = v1 - v2b + apply(b_ref, f2)
    i3a = i2 - apply(a_ref, v2b - v2a)
    i3b = apply(a_ref, v2b)
    v3c = apply(b_ref, i3b)
    v3a = v2a - apply(b_ref, i3a - f3)
    v3b = v2b - v3c + apply(b_ref, i3a)
    sub8 = iota((8, 128), 0)
    for c in range(32):
        row = slice(c, c + 1)
        add = jnp.where(sub8 == 0, v3a[row], jnp.where(sub8 == 1, v3b[row], jnp.where(sub8 == 2, v3c[row], 0.0)))
        vo_ref[c] = v_ref[c] + add
        add = jnp.where(sub8 == 0, i3a[row], jnp.where(sub8 == 1, i3b[row], 0.0))
        io_ref[c] = i_ref[c] + add
    mean_a = jnp.sum(i3a, axis=0, keepdims=True) * (1.0 / 32.0)
    mean_b = jnp.sum(i3b, axis=0, keepdims=True) * (1.0 / 32.0)
    indo_ref[...] = ind_ref[...]
    indo_ref[0:8, :] = ind_ref[0:8, :] + jnp.where(sub8 == 0, mean_a, jnp.where(sub8 == 1, mean_b, 0.0))


def junctions(ends, link, inductance, capacitance, volts, amps, induced):
    head = pl.BlockSpec((32, 8, 128), lambda n: (0, 0, 0))
    whole = lambda *dims: pl.BlockSpec(dims, lambda n: (0,) * len(dims))
    return call(
        junction_kernel,
        (shape(32, 128, 128), shape(32, 128, 128), shape(128, 128)),
        ends, link, inductance, capacitance, volts, amps, induced,
        name="junctions",
        grid=(1,),
        in_specs=[whole(3, 32, 128), whole(1, 128), whole(32, 32, 128), whole(32, 32, 128), head, head, whole(128, 128)],
        out_specs=(head, head, whole(128, 128)),
        aliases={4: 0, 5: 1},
        scratch=[pltpu.VMEM((32, 128), F)],
        limit=16,
    )


def magnetic_kernel(e_ref, h_ref, above_ref, ho_ref, layer_ref):
    sub = iota((8, 256), 0)
    lane = iota((8, 256), 1)

    def one_layer(x, carry):
        nx = jnp.minimum(x + 1, 7)
        last = x == 7
        for yb in range(16):
            rows = slice(8 * yb, 8 * yb + 8)
            e = [e_ref[k, x, rows, :] for k in range(3)]
            ahead = [jnp.where(last, above_ref[k, rows, :], e_ref[k + 1, nx, rows, :]) for k in range(2)]

            def diff_y(k):
                rolled = pltpu.roll(e[k], 7, 0)
                edge = e_ref[k, x, 8 * yb + 8 : 8 * yb + 9, :] if yb < 15 else jnp.zeros((1, 256), F)
                return jnp.where(sub == 7, edge, rolled) - e[k]

            def diff_z(k):
                return jnp.where(lane == 255, 0.0, pltpu.roll(e[k], 255, 1)) - e[k]

            curl = (
                diff_y(2) - diff_z(1),
                diff_z(0) - (ahead[1] - e[2]),
                (ahead[0] - e[1]) - diff_y(0),
            )
            for k in range(3):
                ho_ref[k, x, rows, :] = h_ref[k, x, rows, :] - COURANT * curl[k]
        return carry

    lax.fori_loop(0, 8, one_layer, 0)
    layer_ref[...] = ho_ref[1:3, 7]


def magnetics(electric, magnetic, above):
    return call(
        magnetic_kernel,
        (shape(3, 8, 128, 256), shape(2, 128, 256)),
        electric, magnetic, above,
        name="magnetics",
        limit=24,
    )


def sort_columns(keys):
    sub8 = iota((8, 128), 0)
    keys = list(keys)
    size = 2
    while size <= 128:
        stride = size // 2
        while stride >= 1:
            if stride >= 8:
                gap = stride // 8
                for n in range(16):
                    if n & gap:
                        continue
                    rising = ((n * 8) & size) == 0 or size == 128
                    low = jnp.minimum(keys[n], keys[n + gap])
                    high = jnp.maximum(keys[n], keys[n + gap])
                    keys[n], keys[n + gap] = (low, high) if rising else (high, low)
            else:
                partner = sub8 ^ stride
                first = (sub8 & stride) == 0
                for n in range(16):
                    other = take(keys[n], partner, 0)
                    if size >= 8:
                        rising = ((n * 8) & size) == 0 or size == 128
                        want_low = first if rising else ~first
                    else:
                        want_low = ((sub8 & size) == 0) == first
                    keys[n] = jnp.where(want_low, jnp.minimum(keys[n], other), jnp.maximum(keys[n], other))
            stride //= 2
        size *= 2
    return keys


def electric_kernel(
    e_ref, h_ref, below_ref, sigma_ref, ind_ref, tan_ref, idx_ref,
    eo_ref, cell_s, perm_s, val_s, dep_s, plane_s,
):
    sub8 = iota((8, 128), 0)
    lane8 = iota((8, 128), 1)
    keys = []
    for n in range(16):
        owner = sub8 + 8 * n
        cell = idx_ref[8 * n : 8 * n + 8, :]
        keys.append(((owner & 1) * 1024 + cell) * 128 + owner)
    keys = jnp.concatenate(sort_columns(keys), 0).T
    cell_s[...] = keys >> 7
    perm_s[...] = keys & 127

    for k in range(3):
        val_s[k] = (tan_ref[k] * ind_ref[...]).T
    for n in range(16):
        rows = slice(8 * n, 8 * n + 8)
        perm = perm_s[rows, :]
        cell = cell_s[rows, :]
        val = [take(val_s[k, rows, :], perm, 1) for k in range(3)]
        for gap in (1, 2, 4, 8, 16, 32):
            same = pltpu.roll(cell, gap, 1) == cell
            val = [v + jnp.where(same, pltpu.roll(v, gap, 1), 0.0) for v in val]
        for k in range(3):
            val_s[k, rows, :] = val[k]

    def spread(n, carry):
        rows = pl.ds(pl.multiple_of(n * 8, 8), 8)
        cell = cell_s[rows, :]
        val = [val_s[k, rows, :] for k in range(3)]
        for h in range(2):
            fence = {
                p: take(cell, jnp.full((8, 128), 64 * h + p, I32), 1)
                for p in (0, 8, 16, 24, 32, 40, 48, 56)
            }
            for x in range(8):
                target = lane8 + (h * 1024 + x * 128)
                up = fence[32] <= target
                pos = jnp.where(up, 64 * h + 32, 64 * h)
                cur = jnp.where(up, fence[32], fence[0])
                probe = jnp.where(up, fence[48], fence[16])
                up2 = probe <= target
                pos = jnp.where(up2, pos + 16, pos)
                cur = jnp.where(up2, probe, cur)
                probe = jnp.where(
                    up,
                    jnp.where(up2, fence[56], fence[40]),
                    jnp.where(up2, fence[24], fence[8]),
                )
                hit = probe <= target
                pos = jnp.where(hit, pos + 8, pos)
                cur = jnp.where(hit, probe, cur)
                for step in (4, 2, 1):
                    probe = take(cell, pos + step, 1)
                    hit = probe <= target
                    pos = jnp.where(hit, pos + step, pos)
                    cur = jnp.where(hit, probe, cur)
                found = cur == target
                for k in range(3):
                    dep_s[h, k, x, rows, :] = jnp.where(found, take(val[k], pos, 1), 0.0)
        return carry

    lax.fori_loop(0, 16, spread, 0)

    sub = iota((8, 256), 0)
    lane = iota((8, 256), 1)

    def one_layer(x, carry):
        px = jnp.maximum(x - 1, 0)
        first = x == 0
        for k in range(3):
            for h in range(2):
                plane_s[k, :, 128 * h : 128 * h + 128] = dep_s[h, k, x].T
        for yb in range(16):
            rows = slice(8 * yb, 8 * yb + 8)
            m = [h_ref[k, x, rows, :] for k in range(3)]
            behind = [jnp.where(first, below_ref[k, rows, :], h_ref[k + 1, px, rows, :]) for k in range(2)]

            def diff_y(k):
                rolled = pltpu.roll(m[k], 1, 0)
                edge = h_ref[k, x, 8 * yb - 1 : 8 * yb, :] if yb > 0 else jnp.zeros((1, 256), F)
                return m[k] - jnp.where(sub == 0, edge, rolled)

            def diff_z(k):
                return m[k] - jnp.where(lane == 0, 0.0, pltpu.roll(m[k], 1, 1))

            curl = (
                diff_y(2) - diff_z(1),
                diff_z(0) - (m[2] - behind[1]),
                (m[1] - behind[0]) - diff_y(0),
            )
            sigma = sigma_ref[x, rows, :]
            inverse = 1.0 / (1.0 + sigma)
            keep = (1.0 - sigma) * inverse
            push = COURANT * inverse
            for k in range(3):
                eo_ref[k, x, rows, :] = keep * e_ref[k, x, rows, :] + push * (curl[k] - plane_s[k, rows, :])
        return carry

    lax.fori_loop(0, 8, one_layer, 0)


def electrics(electric, magnetic_new, below, conductivity, induced, tangent, cells):
    return call(
        electric_kernel,
        shape(3, 8, 128, 256),
        electric, magnetic_new, below, conductivity, induced, tangent, cells,
        name="electrics",
        scratch=[
            pltpu.VMEM((128, 128), I32),
            pltpu.VMEM((128, 128), I32),
            pltpu.VMEM((3, 128, 128), F),
            pltpu.VMEM((2, 3, 8, 128, 128), F),
            pltpu.VMEM((3, 128, 256), F),
        ],
        limit=30,
    )


BOTH = ("slab", "cable")


def along(x, axis, by):
    peers = lax.axis_size(axis)
    return lax.ppermute(x, axis, [(i, i + by) for i in range(peers) if 0 <= i + by < peers])


def around(x, axis):
    peers = lax.axis_size(axis)
    return lax.ppermute(x, axis, [(i, (i + 1) % peers) for i in range(peers)])


def exchange(x):
    return lax.all_to_all(x, BOTH, split_axis=0, concat_axis=0, tiled=True)


def local(
    electric, magnetic, conductivity, voltage, current, inverse_inductance,
    inverse_capacitance, tangent, sample_cell, tube_length, junction_link,
):
    cells = sample_cell.reshape(128, 128)
    steer = tangent.reshape(3, 128, 128)
    drive_local, layer = call(
        gather_kernel, (shape(128, 128), shape(2, 128, 256)), electric, cells, steer, name="gather", limit=20
    )
    above = along(layer, BOTH, -1)
    drive = exchange(drive_local)
    volts, amps, ends, induced = lines(
        voltage, current, inverse_inductance, inverse_capacitance, drive, tube_length.reshape(1, 128)
    )
    ends = around(ends, "cable")
    magnetic_new, layer = magnetics(electric, magnetic, above)
    below = along(layer, BOTH, 1)
    volts, amps, induced = junctions(
        ends, junction_link.reshape(1, 128), inverse_inductance, inverse_capacitance, volts, amps, induced
    )
    induced_local = exchange(induced)
    electric_new = electrics(electric, magnetic_new, below, conductivity, induced_local, steer, cells)
    return electric_new, magnetic_new, volts, amps


def solution(mesh):
    grid = P(None, BOTH, None, None)
    tubes = P(None, None, BOTH)
    return jax.shard_map(
        local,
        mesh=mesh,
        in_specs=(
            grid, grid, P(BOTH, None, None), tubes, tubes, tubes, tubes,
            P(None, BOTH, None), P(BOTH, None), P(BOTH), P(BOTH),
        ),
        out_specs=(grid, grid, tubes, tubes),
        check_vma=False,
    )
```

```python
import jax
import jax.numpy as jnp
from jax import lax
from jax.experimental import pallas as pl
from jax.experimental.pallas import tpu as pltpu
from jax.sharding import PartitionSpec as P

F = jnp.float32
B16 = jnp.bfloat16
I32 = jnp.int32
SUB = 3
COURANT = 0.5
MB = 2**20


def take(x, index, axis):
    return jnp.take_along_axis(x, index, axis=axis, mode="promise_in_bounds")


def iota(shape, axis):
    return lax.broadcasted_iota(I32, shape, axis)


def call(body, out, *ins, name, scratch=(), limit=40, in_specs=None, aliases=None, out_specs=None, micros=None, grid=()):
    kw = {}
    if in_specs is not None:
        kw["in_specs"] = in_specs
    if out_specs is not None:
        kw["out_specs"] = out_specs
    return pl.pallas_call(
        body,
        out_shape=out,
        grid=grid,
        scratch_shapes=list(scratch),
        input_output_aliases=aliases or {},
        compiler_params=pltpu.CompilerParams(vmem_limit_bytes=limit * MB),
        cost_estimate=pl.CostEstimate(flops=0, bytes_accessed=int(micros * 3.69e6), transcendentals=0) if micros else None,
        name=name,
        **kw,
    )(*ins)


def shape(*dims, dtype=F):
    return jax.ShapeDtypeStruct(dims, dtype)


def gather_kernel(e_hbm, idx_hbm, tan_hbm, drive_ref, layer_ref, e_ref, idx_ref, tan_ref, sems):
    copies = [pltpu.make_async_copy(e_hbm.at[:, x], e_ref.at[:, x], sems.at[x]) for x in range(8)]
    idx_copy = pltpu.make_async_copy(idx_hbm, idx_ref, sems.at[8])
    tan_copy = pltpu.make_async_copy(tan_hbm, tan_ref, sems.at[9])
    idx_copy.start()
    for copy in copies:
        copy.start()
    tan_copy.start()
    idx_copy.wait()
    for h in range(2):
        lanes = pl.ds(h * 128, 128)
        rows = pl.ds(h, 64, stride=2)
        idx = idx_ref[rows, :]
        idx = [idx[8 * g : 8 * g + 8] for g in range(8)]
        low = [i & 7 for i in idx]
        high = [i >> 3 for i in idx]
        acc = (jnp.zeros((8, 128), F),) * 24
        for x in range(8):
            if h == 0:
                copies[x].wait()

            def step(yb, acc):
                acc = list(acc)
                yrows = pl.ds(pl.multiple_of(yb * 8, 8), 8)
                src = [e_ref[k, x, yrows, lanes] for k in range(3)]
                for g in range(8):
                    hit = high[g] == yb + 16 * x
                    for k in range(3):
                        acc[g * 3 + k] = jnp.where(hit, take(src[k], low[g], 0), acc[g * 3 + k])
                return tuple(acc)

            acc = lax.fori_loop(0, 16, step, acc, unroll=4)
        if h == 0:
            tan_copy.wait()
            layer_ref[...] = e_ref[1:3, 0]
        picked = [jnp.concatenate([acc[g * 3 + k] for g in range(8)], 0) for k in range(3)]
        steer = [tan_ref[k, rows, :] for k in range(3)]
        drive_ref[rows, :] = steer[0] * picked[0] + steer[1] * picked[1] + steer[2] * picked[2]


def samples(electric, cells, steer):
    return call(
        gather_kernel,
        (shape(128, 128), shape(2, 128, 256)),
        electric, cells, steer,
        name="samples",
        in_specs=[pl.BlockSpec(memory_space=pltpu.HBM)] * 3,
        scratch=[
            pltpu.VMEM((3, 8, 128, 256), F),
            pltpu.VMEM((128, 128), I32),
            pltpu.VMEM((3, 128, 128), F),
            pltpu.SemaphoreType.DMA((10,)),
        ],
        limit=58,
        micros=4,
    )


def merge_pair(x, y):
    low = iota((8, 128), 0) < 4
    return jnp.where(low, x, pltpu.roll(y, 4, 0)), jnp.where(low, pltpu.roll(x, 4, 0), y)


def split_parts(x):
    high = x.astype(B16)
    return high, (x - high.astype(F)).astype(B16)


def line_kernel(
    v_hbm, i_hbm, a_hbm, b_hbm, drive_ref, len_ref,
    vo_hbm, io_hbm, ends_ref, ind_ref,
    vt, it, at, vg, ig, ah, bh, dg, eg, indt, v_ref, i_ref, a_ref, b_ref, sems, in_sems,
):
    arrivals = []
    for q in range(4):
        part = pl.ds(8 * q, 8)
        pair = [
            pltpu.make_async_copy(src.at[part], dst.at[part], in_sems.at[2 * q + m])
            for m, (src, dst) in enumerate(((v_hbm, v_ref), (i_hbm, i_ref)))
        ]
        for copy in pair:
            copy.start()
        arrivals.append(pair)
    matrices = [
        pltpu.make_async_copy(src, dst, in_sems.at[8 + m])
        for m, (src, dst) in enumerate(((a_hbm, a_ref), (b_hbm, b_ref)))
    ]
    for copy in matrices:
        copy.start()
    sub8 = iota((8, 128), 0)
    lane8 = iota((8, 128), 1)
    lane = iota((128, 128), 1)

    def turn_in(c, carry):
        vt[c] = v_ref[c].T
        it[c] = i_ref[c].T
        return carry

    for q in range(4):
        for copy in arrivals[q]:
            copy.wait()
        lax.fori_loop(8 * q, 8 * q + 8, turn_in, 0, unroll=4)
    for copy in matrices:
        copy.wait()

    spread = [(sub8 >> 2) + 2 * j for j in range(4)]
    own = (sub8 & 3) == (lane8 & 3)
    for m_ref, dst in ((a_ref, ah), (b_ref, bh)):

        def expand(c, carry):
            tiles = []
            for q in range(4):
                tile = m_ref[c, 8 * q : 8 * q + 8, :]
                for j in range(4):
                    tiles.append(jnp.where(own, take(tile, spread[j], 0), 0.0))
            at[c] = jnp.concatenate(tiles, 0).T
            return carry

        lax.fori_loop(0, 32, expand, 0, unroll=4)

        def pack(b, carry):
            rows = pl.ds(pl.multiple_of(b * 8, 8), 8)
            first, second = [], []
            for i in range(16):
                g0, g1 = merge_pair(at[2 * i, rows, :], at[2 * i + 1, rows, :])
                first.append(g0)
                second.append(g1)
            for p, tiles in enumerate((first, second)):
                high, low = split_parts(jnp.concatenate(tiles, 0))
                out_rows = pl.ds(pl.multiple_of(b * 256 + p * 128, 128), 128)
                dst[out_rows, 0:128] = high
                dst[out_rows, 128:256] = low
            return carry

        lax.fori_loop(0, 16, pack, 0, unroll=2)

    def regroup(b, carry):
        rows = pl.ds(pl.multiple_of(b * 8, 8), 8)
        for src, dst in ((vt, vg), (it, ig)):
            for i in range(16):
                g0, g1 = merge_pair(src[2 * i, rows, :], src[2 * i + 1, rows, :])
                dst[pl.ds(pl.multiple_of(b * 256 + 8 * i, 8), 8), :] = g0
                dst[pl.ds(pl.multiple_of(b * 256 + 128 + 8 * i, 8), 8), :] = g1
        return carry

    lax.fori_loop(0, 16, regroup, 0, unroll=2)

    at[0] = drive_ref[...].T
    at[1] = jnp.broadcast_to(len_ref[...].astype(F), (128, 128)).T
    for b in range(16):
        rows = slice(8 * b, 8 * b + 8)
        for p, value in enumerate(merge_pair(at[0, rows, :], at[0, rows, :])):
            dg[16 * b + 8 * p : 16 * b + 8 * p + 8, :] = value
        for p, value in enumerate(merge_pair(at[1, rows, :], at[1, rows, :])):
            eg[16 * b + 8 * p : 16 * b + 8 * p + 8, :] = value.astype(I32)

    def product(m_ref, rows, x):
        high, low = split_parts(x)
        rhs = jnp.concatenate([high, low], 1)
        rhs = jnp.concatenate([rhs, rhs], 0)
        y = jnp.dot(m_ref[rows, :], rhs, preferred_element_type=F)
        return y[:, :128] + y[:, 128:]

    unroll = 16
    for substep in range(SUB):

        def current_step(n, acc):
            for u in range(unroll):
                g = n * unroll + u
                rows = pl.ds(pl.multiple_of(g * 128, 128), 128)
                small = pl.ds(pl.multiple_of(g * 8, 8), 8)
                length = eg[small, :]
                live = jnp.concatenate([lane8 < length] * 16, 0)
                drive = jnp.concatenate([dg[small, :]] * 16, 0)
                volts = vg[rows, :]
                ahead = jnp.where(lane == 127, 0.0, pltpu.roll(volts, 127, 1))
                y = product(ah, rows, ahead - volts - drive)
                amps = jnp.where(live, ig[rows, :] - y, 0.0)
                ig[rows, :] = amps
                spot = lane8 == 4 * g + (sub8 & 3)
                acc = tuple(
                    jnp.where(spot, take(amps[8 * i : 8 * i + 8], length - 1, 1), acc[i])
                    for i in range(16)
                )
            return acc

        acc = lax.fori_loop(0, 32 // unroll, current_step, (jnp.zeros((8, 128), F),) * 16)
        pick = (sub8 & 1) * 4 + (lane8 & 3)
        for q in range(4):
            out = take(acc[4 * q], pick, 0)
            for i in range(1, 4):
                out = jnp.where((sub8 >> 1) == i, take(acc[4 * q + i], pick, 0), out)
            ends_ref[substep, 8 * q : 8 * q + 8, :] = out

        def voltage_step(n, carry):
            for u in range(unroll):
                g = n * unroll + u
                rows = pl.ds(pl.multiple_of(g * 128, 128), 128)
                small = pl.ds(pl.multiple_of(g * 8, 8), 8)
                live = jnp.concatenate([lane8 < eg[small, :]] * 16, 0)
                amps = ig[rows, :]
                behind = jnp.where(lane == 0, 0.0, pltpu.roll(amps, 1, 1))
                y = product(bh, rows, amps - behind)
                vg[rows, :] = jnp.where(live, vg[rows, :] - y, 0.0)
            return carry

        lax.fori_loop(0, 32 // unroll, voltage_step, 0)

    def ungroup(b, carry):
        rows = pl.ds(pl.multiple_of(b * 8, 8), 8)
        for src, dst in ((vg, vt), (ig, it)):
            sums = [None, None]
            for i in range(16):
                g0 = src[pl.ds(pl.multiple_of(b * 256 + 8 * i, 8), 8), :]
                g1 = src[pl.ds(pl.multiple_of(b * 256 + 128 + 8 * i, 8), 8), :]
                c0, c1 = merge_pair(g0, g1)
                dst[2 * i, rows, :] = c0
                dst[2 * i + 1, rows, :] = c1
                if src is ig:
                    sums = [c0 + c1 if s is None else s + c0 + c1 for s in sums[:1]] + [None]
            if src is ig:
                indt[rows, :] = sums[0] * (1.0 / 32.0)
        return carry

    lax.fori_loop(0, 16, ungroup, 0, unroll=2)

    ind_ref[...] = indt[...].T
    copies = []
    for q in range(4):

        def turn_out(n, carry):
            c = 8 * q + n
            vg[pl.ds(pl.multiple_of(c * 128, 128), 128), :] = vt[c].T
            ig[pl.ds(pl.multiple_of(c * 128, 128), 128), :] = it[c].T
            return carry

        lax.fori_loop(0, 8, turn_out, 0, unroll=4)
        part = pl.ds(1024 * q, 1024)
        for m, (src, dst) in enumerate(((vg, vo_hbm), (ig, io_hbm))):
            copy = pltpu.make_async_copy(src.at[part], dst.at[part], sems.at[2 * q + m])
            copy.start()
            copies.append(copy)
    for copy in copies:
        copy.wait()


def lines(voltage, current, inductance, capacitance, drive, lengths):
    big = pltpu.VMEM((32, 128, 128), F)
    flat = pltpu.VMEM((4096, 128), F)
    packed = pltpu.VMEM((4096, 256), B16)
    outside = pl.BlockSpec(memory_space=pltpu.HBM)
    inside = pl.BlockSpec(memory_space=pltpu.VMEM)
    volts, amps, ends, induced = call(
        line_kernel,
        (shape(4096, 128), shape(4096, 128), shape(3, 32, 128), shape(128, 128)),
        voltage, current, inductance, capacitance, drive, lengths,
        name="lines",
        in_specs=[outside] * 4 + [inside] * 2,
        out_specs=(outside, outside, inside, inside),
        scratch=[big, big, big, flat, flat, packed, packed, pltpu.VMEM((256, 128), F),
                 pltpu.VMEM((256, 128), I32), pltpu.VMEM((128, 128), F), big, big,
                 pltpu.VMEM((32, 32, 128), F), pltpu.VMEM((32, 32, 128), F),
                 pltpu.SemaphoreType.DMA((8,)), pltpu.SemaphoreType.DMA((10,))],
        limit=53,
        micros=18,
    )
    return volts.reshape(32, 128, 128), amps.reshape(32, 128, 128), ends, induced


def junction_kernel(ends_ref, link_ref, a_ref, b_ref, ind_ref, fix_ref, indo_ref, buf):
    link = jnp.broadcast_to(link_ref[...], (8, 128))
    inflow = [
        jnp.concatenate([take(ends_ref[k, 8 * q : 8 * q + 8, :], link, 1) for q in range(4)], 0)
        for k in range(SUB)
    ]

    def apply(m_ref, x):
        buf[...] = x
        parts = [None] * 4
        for d in range(32):
            term = m_ref[d] * buf[d : d + 1, :]
            parts[d % 4] = term if parts[d % 4] is None else parts[d % 4] + term
        return (parts[0] + parts[1]) + (parts[2] + parts[3])

    f1, f2, f3 = inflow
    v1 = apply(b_ref, f1)
    i2 = apply(a_ref, v1)
    v2b = apply(b_ref, i2)
    v2a = v1 - v2b + apply(b_ref, f2)
    i3a = i2 - apply(a_ref, v2b - v2a)
    i3b = apply(a_ref, v2b)
    v3c = apply(b_ref, i3b)
    v3a = v2a - apply(b_ref, i3a - f3)
    v3b = v2b - v3c + apply(b_ref, i3a)
    sub8 = iota((8, 128), 0)
    for n, value in enumerate((v3a, v3b, v3c, i3a, i3b)):
        fix_ref[n] = value
    mean_a = jnp.sum(i3a, axis=0, keepdims=True) * (1.0 / 32.0)
    mean_b = jnp.sum(i3b, axis=0, keepdims=True) * (1.0 / 32.0)
    indo_ref[...] = ind_ref[...]
    indo_ref[0:8, :] = ind_ref[0:8, :] + jnp.where(sub8 == 0, mean_a, jnp.where(sub8 == 1, mean_b, 0.0))


def junctions(ends, link, inductance, capacitance, induced):
    return call(
        junction_kernel,
        (shape(5, 32, 128), shape(128, 128)),
        ends, link, inductance, capacitance, induced,
        name="junctions",
        scratch=[pltpu.VMEM((32, 128), F)],
        limit=3,
        micros=1,
    )


def finish_kernel(v_ref, i_ref, fix_ref, vo_ref, io_ref):
    sub8 = iota((8, 128), 0)
    for c in range(32):
        fix = [fix_ref[m, c : c + 1, :] for m in range(5)]
        first, second = sub8 == 0, sub8 == 1
        vo_ref[c] = v_ref[c] + jnp.where(first, fix[0], jnp.where(second, fix[1], jnp.where(sub8 == 2, fix[2], 0.0)))
        io_ref[c] = i_ref[c] + jnp.where(first, fix[3], jnp.where(second, fix[4], 0.0))


def finish(volts, amps, fix):
    head = pl.BlockSpec((32, 8, 128), lambda n: (0, 0, 0))
    return call(
        finish_kernel,
        (shape(32, 128, 128), shape(32, 128, 128)),
        volts, amps, fix,
        name="finish",
        grid=(1,),
        in_specs=[head, head, pl.BlockSpec((5, 32, 128), lambda n: (0, 0, 0))],
        out_specs=(head, head),
        aliases={0: 0, 1: 1},
        limit=8,
        micros=2,
    )


def magnetic_kernel(e_hbm, h_hbm, above_ref, ho_hbm, layer_ref, e_ref, h_ref, ho_ref, sems):
    sub = iota((8, 256), 0)
    lane = iota((8, 256), 1)

    def fetch(x):
        return (
            pltpu.make_async_copy(e_hbm.at[:, x], e_ref.at[:, x], sems.at[0, x]),
            pltpu.make_async_copy(h_hbm.at[:, x], h_ref.at[:, x], sems.at[1, x]),
        )

    def store(x):
        return pltpu.make_async_copy(ho_ref.at[:, x], ho_hbm.at[:, x], sems.at[2, x])

    for x in range(8):
        for copy in fetch(x):
            copy.start()
    fetch(0)[0].wait()

    def one_layer(x, carry):
        nx = jnp.minimum(x + 1, 7)
        last = x == 7
        for yb in range(16):
            rows = slice(8 * yb, 8 * yb + 8)
            e = [e_ref[k, x, rows, :] for k in range(3)]
            ahead = [jnp.where(last, above_ref[k, rows, :], e_ref[k + 1, nx, rows, :]) for k in range(2)]

            def diff_y(k):
                rolled = pltpu.roll(e[k], 7, 0)
                edge = e_ref[k, x, 8 * yb + 8 : 8 * yb + 9, :] if yb < 15 else jnp.zeros((1, 256), F)
                return jnp.where(sub == 7, edge, rolled) - e[k]

            def diff_z(k):
                return jnp.where(lane == 255, 0.0, pltpu.roll(e[k], 255, 1)) - e[k]

            curl = (
                diff_y(2) - diff_z(1),
                diff_z(0) - (ahead[1] - e[2]),
                (ahead[0] - e[1]) - diff_y(0),
            )
            for k in range(3):
                ho_ref[k, x, rows, :] = h_ref[k, x, rows, :] - COURANT * curl[k]
        return carry

    def layer_step(x, carry):
        @pl.when(x < 7)
        def _():
            fetch(x + 1)[0].wait()

        fetch(x)[1].wait()
        one_layer(x, carry)
        store(x).start()
        return carry

    lax.fori_loop(0, 8, layer_step, 0)
    layer_ref[...] = ho_ref[1:3, 7]
    for x in range(8):
        store(x).wait()


def magnetics(electric, magnetic, above):
    whole = pltpu.VMEM((3, 8, 128, 256), F)
    outside = pl.BlockSpec(memory_space=pltpu.HBM)
    inside = pl.BlockSpec(memory_space=pltpu.VMEM)
    return call(
        magnetic_kernel,
        (shape(3, 8, 128, 256), shape(2, 128, 256)),
        electric, magnetic, above,
        name="magnetics",
        in_specs=[outside, outside, inside],
        out_specs=(outside, inside),
        scratch=[whole, whole, whole, pltpu.SemaphoreType.DMA((3, 8))],
        limit=53,
        micros=4,
    )


def sort_columns(keys):
    sub8 = iota((8, 128), 0)
    keys = list(keys)
    size = 2
    while size <= 128:
        stride = size // 2
        while stride >= 1:
            if stride >= 8:
                gap = stride // 8
                for n in range(16):
                    if n & gap:
                        continue
                    rising = ((n * 8) & size) == 0 or size == 128
                    low = jnp.minimum(keys[n], keys[n + gap])
                    high = jnp.maximum(keys[n], keys[n + gap])
                    keys[n], keys[n + gap] = (low, high) if rising else (high, low)
            else:
                partner = sub8 ^ stride
                first = (sub8 & stride) == 0
                for n in range(16):
                    other = take(keys[n], partner, 0)
                    if size >= 8:
                        rising = ((n * 8) & size) == 0 or size == 128
                        want_low = first if rising else ~first
                    else:
                        want_low = ((sub8 & size) == 0) == first
                    keys[n] = jnp.where(want_low, jnp.minimum(keys[n], other), jnp.maximum(keys[n], other))
            stride //= 2
        size *= 2
    return keys


def search_kernel(idx_ref, cell_ref, perm_ref, pos_ref):
    sub8 = iota((8, 128), 0)
    lane8 = iota((8, 128), 1)
    keys = []
    for n in range(16):
        owner = sub8 + 8 * n
        cell = idx_ref[8 * n : 8 * n + 8, :]
        keys.append(((owner & 1) * 1024 + cell) * 128 + owner)
    keys = jnp.concatenate(sort_columns(keys), 0).T
    cell_ref[...] = keys >> 7
    perm_ref[...] = keys & 127

    def spread(n, carry):
        rows = pl.ds(pl.multiple_of(n * 8, 8), 8)
        cell = cell_ref[rows, :]
        for h in range(2):
            fence = {
                p: take(cell, jnp.full((8, 128), 64 * h + p, I32), 1)
                for p in (0, 8, 16, 24, 32, 40, 48, 56)
            }
            chains = []
            for x in range(8):
                target = lane8 + (h * 1024 + x * 128)
                up = fence[32] <= target
                pos = jnp.where(up, 64 * h + 32, 64 * h)
                cur = jnp.where(up, fence[32], fence[0])
                probe = jnp.where(up, fence[48], fence[16])
                up2 = probe <= target
                pos = jnp.where(up2, pos + 16, pos)
                cur = jnp.where(up2, probe, cur)
                probe = jnp.where(
                    up,
                    jnp.where(up2, fence[56], fence[40]),
                    jnp.where(up2, fence[24], fence[8]),
                )
                hit = probe <= target
                chains.append((target, jnp.where(hit, pos + 8, pos), jnp.where(hit, probe, cur)))
            for step in (4, 2, 1):
                probes = [take(cell, pos + step, 1) for _, pos, _ in chains]
                hits = [probe <= chain[0] for probe, chain in zip(probes, chains)]
                chains = [
                    (target, jnp.where(hit, pos + step, pos), jnp.where(hit, probe, cur))
                    for (target, pos, cur), probe, hit in zip(chains, probes, hits)
                ]
            for x, (target, pos, cur) in enumerate(chains):
                pos_ref[h, x, rows, :] = jnp.where(cur == target, pos, -1)
        return carry

    lax.fori_loop(0, 16, spread, 0)


def search(cells):
    return call(
        search_kernel,
        (shape(128, 128, dtype=I32), shape(128, 128, dtype=I32), shape(2, 8, 128, 128, dtype=I32)),
        cells,
        name="search",
        limit=4,
        micros=4,
    )


def electric_kernel(
    e_hbm, h_hbm, below_ref, sigma_hbm, ind_ref, tan_ref, cell_s, perm_s, pos_hbm,
    eo_hbm, val_s, plane_s, eo_ref, e_ref, h_ref, sigma_ref, pos_ref, sems, in_sems,
):
    def fetch(x):
        return (
            pltpu.make_async_copy(pos_hbm.at[:, x], pos_ref.at[:, x], in_sems.at[0, x]),
            pltpu.make_async_copy(h_hbm.at[:, x], h_ref.at[:, x], in_sems.at[1, x]),
            pltpu.make_async_copy(e_hbm.at[:, x], e_ref.at[:, x], in_sems.at[2, x]),
            pltpu.make_async_copy(sigma_hbm.at[x], sigma_ref.at[x], in_sems.at[3, x]),
        )

    for x in range(8):
        for copy in fetch(x):
            copy.start()
    for k in range(3):
        val_s[k] = (tan_ref[k] * ind_ref[...]).T
    for n in range(16):
        rows = slice(8 * n, 8 * n + 8)
        perm = perm_s[rows, :]
        cell = cell_s[rows, :]
        val = [take(val_s[k, rows, :], perm, 1) for k in range(3)]
        for gap in (1, 2, 4, 8, 16, 32):
            same = pltpu.roll(cell, gap, 1) == cell
            val = [v + jnp.where(same, pltpu.roll(v, gap, 1), 0.0) for v in val]
        for k in range(3):
            val_s[k, rows, :] = val[k]

    sub = iota((8, 256), 0)
    lane = iota((8, 256), 1)

    def one_layer(x, carry):
        px = jnp.maximum(x - 1, 0)
        first = x == 0
        for h in range(2):
            tiles = [[], [], []]
            for n in range(16):
                pos = pos_ref[h, x, 8 * n : 8 * n + 8, :]
                spot = pos & 127
                for k in range(3):
                    picked = take(val_s[k, 8 * n : 8 * n + 8, :], spot, 1)
                    tiles[k].append(jnp.where(pos >= 0, picked, 0.0))
            for k in range(3):
                plane_s[k, :, 128 * h : 128 * h + 128] = jnp.concatenate(tiles[k], 0).T
        for yb in range(16):
            rows = slice(8 * yb, 8 * yb + 8)
            m = [h_ref[k, x, rows, :] for k in range(3)]
            behind = [jnp.where(first, below_ref[k, rows, :], h_ref[k + 1, px, rows, :]) for k in range(2)]

            def diff_y(k):
                rolled = pltpu.roll(m[k], 1, 0)
                edge = h_ref[k, x, 8 * yb - 1 : 8 * yb, :] if yb > 0 else jnp.zeros((1, 256), F)
                return m[k] - jnp.where(sub == 0, edge, rolled)

            def diff_z(k):
                return m[k] - jnp.where(lane == 0, 0.0, pltpu.roll(m[k], 1, 1))

            curl = (
                diff_y(2) - diff_z(1),
                diff_z(0) - (m[2] - behind[1]),
                (m[1] - behind[0]) - diff_y(0),
            )
            sigma = sigma_ref[x, rows, :]
            inverse = 1.0 / (1.0 + sigma)
            keep = (1.0 - sigma) * inverse
            push = COURANT * inverse
            for k in range(3):
                eo_ref[k, x, rows, :] = keep * e_ref[k, x, rows, :] + push * (curl[k] - plane_s[k, rows, :])
        return carry

    def send_layer(x, carry):
        for copy in fetch(x):
            copy.wait()
        one_layer(x, carry)
        pltpu.make_async_copy(eo_ref.at[:, x], eo_hbm.at[:, x], sems.at[x]).start()
        return carry

    lax.fori_loop(0, 8, send_layer, 0)
    for x in range(8):
        pltpu.make_async_copy(eo_ref.at[:, x], eo_hbm.at[:, x], sems.at[x]).wait()


def electrics(electric, magnetic_new, below, conductivity, induced, tangent, found):
    whole = pltpu.VMEM((3, 8, 128, 256), F)
    outside = pl.BlockSpec(memory_space=pltpu.HBM)
    inside = pl.BlockSpec(memory_space=pltpu.VMEM)
    return call(
        electric_kernel,
        shape(3, 8, 128, 256),
        electric, magnetic_new, below, conductivity, induced, tangent, *found,
        name="electrics",
        in_specs=[outside, outside, inside, outside, inside, inside, inside, inside, outside],
        out_specs=outside,
        scratch=[
            pltpu.VMEM((3, 128, 128), F),
            pltpu.VMEM((3, 128, 256), F),
            whole, whole, whole,
            pltpu.VMEM((8, 128, 256), F),
            pltpu.VMEM((2, 8, 128, 128), I32),
            pltpu.SemaphoreType.DMA((8,)),
            pltpu.SemaphoreType.DMA((4, 8)),
        ],
        limit=53,
        micros=6,
    )


BOTH = ("slab", "cable")


def along(x, axis, by):
    peers = lax.axis_size(axis)
    return lax.ppermute(x, axis, [(i, i + by) for i in range(peers) if 0 <= i + by < peers])


def around(x, axis):
    peers = lax.axis_size(axis)
    return lax.ppermute(x, axis, [(i, (i + 1) % peers) for i in range(peers)])


def exchange(x):
    return lax.all_to_all(x, BOTH, split_axis=0, concat_axis=0, tiled=True)


def local(
    electric, magnetic, conductivity, voltage, current, inverse_inductance,
    inverse_capacitance, tangent, sample_cell, tube_length, junction_link,
):
    cells = sample_cell.reshape(128, 128)
    steer = tangent.reshape(3, 128, 128)
    drive_local, layer = samples(electric, cells, steer)
    above = along(layer, BOTH, -1)
    drive = exchange(drive_local)
    magnetic_new, layer = magnetics(electric, magnetic, above)
    drive, layer = lax.optimization_barrier((drive, layer))
    below = along(layer, BOTH, 1)
    volts, amps, ends, induced = lines(
        voltage, current, inverse_inductance, inverse_capacitance, drive, tube_length.reshape(1, 128)
    )
    ends, cells = lax.optimization_barrier((ends, cells))
    ends = around(ends, "cable")
    found = search(cells)
    fix, induced = junctions(
        ends, junction_link.reshape(1, 128), inverse_inductance, inverse_capacitance, induced
    )
    induced, found = lax.optimization_barrier((induced, found))
    induced_local = exchange(induced)
    volts, amps = finish(volts, amps, fix)
    electric_new = electrics(electric, magnetic_new, below, conductivity, induced_local, steer, found)
    return electric_new, magnetic_new, volts, amps


def solution(mesh):
    grid = P(None, BOTH, None, None)
    tubes = P(None, None, BOTH)
    return jax.shard_map(
        local,
        mesh=mesh,
        in_specs=(
            grid, grid, P(BOTH, None, None), tubes, tubes, tubes, tubes,
            P(None, BOTH, None), P(BOTH, None), P(BOTH), P(BOTH),
        ),
        out_specs=(grid, grid, tubes, tubes),
        check_vma=False,
    )
```

```python
import jax
import jax.numpy as jnp
from jax import lax
from jax.experimental import pallas as pl
from jax.experimental.pallas import tpu as pltpu
from jax.sharding import PartitionSpec as P

F = jnp.float32
B16 = jnp.bfloat16
I32 = jnp.int32
SUB = 3
COURANT = 0.5
MB = 2**20


def take(x, index, axis):
    return jnp.take_along_axis(x, index, axis=axis, mode="promise_in_bounds")


def iota(shape, axis):
    return lax.broadcasted_iota(I32, shape, axis)


def call(body, out, *ins, name, scratch=(), limit=40, in_specs=None, aliases=None, out_specs=None, micros=None, grid=()):
    kw = {}
    if in_specs is not None:
        kw["in_specs"] = in_specs
    if out_specs is not None:
        kw["out_specs"] = out_specs
    return pl.pallas_call(
        body,
        out_shape=out,
        grid=grid,
        scratch_shapes=list(scratch),
        input_output_aliases=aliases or {},
        compiler_params=pltpu.CompilerParams(vmem_limit_bytes=limit * MB),
        cost_estimate=pl.CostEstimate(flops=0, bytes_accessed=int(micros * 3.69e6), transcendentals=0) if micros else None,
        name=name,
        **kw,
    )(*ins)


def shape(*dims, dtype=F):
    return jax.ShapeDtypeStruct(dims, dtype)


def gather_kernel(e_hbm, idx_hbm, tan_hbm, drive_ref, layer_ref, e_ref, idx_ref, tan_ref, sems):
    copies = [pltpu.make_async_copy(e_hbm.at[:, x], e_ref.at[:, x], sems.at[x]) for x in range(8)]
    idx_copy = pltpu.make_async_copy(idx_hbm, idx_ref, sems.at[8])
    tan_copy = pltpu.make_async_copy(tan_hbm, tan_ref, sems.at[9])
    idx_copy.start()
    for copy in copies:
        copy.start()
    tan_copy.start()
    idx_copy.wait()
    for h in range(2):
        lanes = pl.ds(h * 128, 128)
        rows = pl.ds(h, 64, stride=2)
        idx = idx_ref[rows, :]
        idx = [idx[8 * g : 8 * g + 8] for g in range(8)]
        low = [i & 7 for i in idx]
        high = [i >> 3 for i in idx]
        acc = (jnp.zeros((8, 128), F),) * 24
        for x in range(8):
            if h == 0:
                copies[x].wait()

            def step(yb, acc):
                acc = list(acc)
                yrows = pl.ds(pl.multiple_of(yb * 8, 8), 8)
                src = [e_ref[k, x, yrows, lanes] for k in range(3)]
                for g in range(8):
                    hit = high[g] == yb + 16 * x
                    for k in range(3):
                        acc[g * 3 + k] = jnp.where(hit, take(src[k], low[g], 0), acc[g * 3 + k])
                return tuple(acc)

            acc = lax.fori_loop(0, 16, step, acc, unroll=4)
        if h == 0:
            tan_copy.wait()
            layer_ref[...] = e_ref[1:3, 0]
        picked = [jnp.concatenate([acc[g * 3 + k] for g in range(8)], 0) for k in range(3)]
        steer = [tan_ref[k, rows, :] for k in range(3)]
        drive_ref[rows, :] = steer[0] * picked[0] + steer[1] * picked[1] + steer[2] * picked[2]


def samples(electric, cells, steer):
    return call(
        gather_kernel,
        (shape(128, 128), shape(2, 128, 256)),
        electric, cells, steer,
        name="samples",
        in_specs=[pl.BlockSpec(memory_space=pltpu.HBM)] * 3,
        scratch=[
            pltpu.VMEM((3, 8, 128, 256), F),
            pltpu.VMEM((128, 128), I32),
            pltpu.VMEM((3, 128, 128), F),
            pltpu.SemaphoreType.DMA((10,)),
        ],
        limit=58,
        micros=4,
    )


def merge_pair(x, y):
    low = iota((8, 128), 0) < 4
    return jnp.where(low, x, pltpu.roll(y, 4, 0)), jnp.where(low, pltpu.roll(x, 4, 0), y)


def split_parts(x):
    high = x.astype(B16)
    return high, (x - high.astype(F)).astype(B16)


def product(m_ref, rows, x):
    high, low = split_parts(x)
    rhs = jnp.concatenate([high, low], 1)
    rhs = jnp.concatenate([rhs, rhs], 0)
    y = jnp.dot(m_ref[rows, :], rhs, preferred_element_type=F)
    return y[:, :128] + y[:, 128:]


def line_kernel(
    v_hbm, i_hbm, a_hbm, b_hbm, drive_ref, len_ref,
    vo_hbm, io_hbm, bo_hbm, eg, ends_ref, ind_ref,
    vt, it, at, vg, ig, ah, bh, dg, indt, v_ref, i_ref, a_ref, b_ref, sems, in_sems,
):
    matrices = [
        pltpu.make_async_copy(src, dst, in_sems.at[8 + m])
        for m, (src, dst) in enumerate(((a_hbm, a_ref), (b_hbm, b_ref)))
    ]
    for copy in matrices:
        copy.start()
    arrivals = []
    for q in range(4):
        part = pl.ds(8 * q, 8)
        pair = [
            pltpu.make_async_copy(src.at[part], dst.at[part], in_sems.at[2 * q + m])
            for m, (src, dst) in enumerate(((v_hbm, v_ref), (i_hbm, i_ref)))
        ]
        for copy in pair:
            copy.start()
        arrivals.append(pair)
    sub8 = iota((8, 128), 0)
    lane8 = iota((8, 128), 1)
    lane = iota((128, 128), 1)


    spread = [(sub8 >> 2) + 2 * j for j in range(4)]
    own = (sub8 & 3) == (lane8 & 3)
    for m_ref, dst, arrival in ((a_ref, ah, matrices[0]), (b_ref, bh, matrices[1])):
        arrival.wait()

        def expand(c, carry):
            tiles = []
            for q in range(4):
                tile = m_ref[c, 8 * q : 8 * q + 8, :]
                for j in range(4):
                    tiles.append(jnp.where(own, take(tile, spread[j], 0), 0.0))
            at[c] = jnp.concatenate(tiles, 0).T
            return carry

        lax.fori_loop(0, 32, expand, 0, unroll=4)

        def pack(b, carry):
            rows = pl.ds(pl.multiple_of(b * 8, 8), 8)
            first, second = [], []
            for i in range(16):
                g0, g1 = merge_pair(at[2 * i, rows, :], at[2 * i + 1, rows, :])
                first.append(g0)
                second.append(g1)
            for p, tiles in enumerate((first, second)):
                high, low = split_parts(jnp.concatenate(tiles, 0))
                out_rows = pl.ds(pl.multiple_of(b * 256 + p * 128, 128), 128)
                dst[out_rows, 0:128] = high
                dst[out_rows, 128:256] = low
            return carry

        lax.fori_loop(0, 16, pack, 0, unroll=2)

    results = [pltpu.make_async_copy(bh, bo_hbm, sems.at[0])]
    results[0].start()

    def turn_in(c, carry):
        vt[c] = v_ref[c].T
        it[c] = i_ref[c].T
        return carry

    for q in range(4):
        for copy in arrivals[q]:
            copy.wait()
        lax.fori_loop(8 * q, 8 * q + 8, turn_in, 0, unroll=4)
    def regroup(b, carry):
        rows = pl.ds(pl.multiple_of(b * 8, 8), 8)
        for src, dst in ((vt, vg), (it, ig)):
            for i in range(16):
                g0, g1 = merge_pair(src[2 * i, rows, :], src[2 * i + 1, rows, :])
                dst[pl.ds(pl.multiple_of(b * 256 + 8 * i, 8), 8), :] = g0
                dst[pl.ds(pl.multiple_of(b * 256 + 128 + 8 * i, 8), 8), :] = g1
        return carry

    lax.fori_loop(0, 16, regroup, 0, unroll=2)

    at[0] = drive_ref[...].T
    at[1] = jnp.broadcast_to(len_ref[...].astype(F), (128, 128)).T
    for b in range(16):
        rows = slice(8 * b, 8 * b + 8)
        for p, value in enumerate(merge_pair(at[0, rows, :], at[0, rows, :])):
            dg[16 * b + 8 * p : 16 * b + 8 * p + 8, :] = value
        for p, value in enumerate(merge_pair(at[1, rows, :], at[1, rows, :])):
            eg[16 * b + 8 * p : 16 * b + 8 * p + 8, :] = value.astype(I32)

    unroll = 16
    for substep in range(SUB):

        def current_step(n, acc):
            for u in range(unroll):
                g = n * unroll + u
                rows = pl.ds(pl.multiple_of(g * 128, 128), 128)
                small = pl.ds(pl.multiple_of(g * 8, 8), 8)
                length = eg[small, :]
                live = jnp.concatenate([lane8 < length] * 16, 0)
                drive = jnp.concatenate([dg[small, :]] * 16, 0)
                volts = vg[rows, :]
                ahead = jnp.where(lane == 127, 0.0, pltpu.roll(volts, 127, 1))
                y = product(ah, rows, ahead - volts - drive)
                amps = jnp.where(live, ig[rows, :] - y, 0.0)
                ig[rows, :] = amps
                spot = lane8 == 4 * g + (sub8 & 3)
                acc = tuple(
                    jnp.where(spot, take(amps[8 * i : 8 * i + 8], length - 1, 1), acc[i])
                    for i in range(16)
                )
            return acc

        acc = lax.fori_loop(0, 32 // unroll, current_step, (jnp.zeros((8, 128), F),) * 16)
        pick = (sub8 & 1) * 4 + (lane8 & 3)
        for q in range(4):
            out = take(acc[4 * q], pick, 0)
            for i in range(1, 4):
                out = jnp.where((sub8 >> 1) == i, take(acc[4 * q + i], pick, 0), out)
            ends_ref[substep, 8 * q : 8 * q + 8, :] = out

        if substep == SUB - 1:
            break

        def voltage_step(n, carry):
            for u in range(unroll):
                g = n * unroll + u
                rows = pl.ds(pl.multiple_of(g * 128, 128), 128)
                small = pl.ds(pl.multiple_of(g * 8, 8), 8)
                live = jnp.concatenate([lane8 < eg[small, :]] * 16, 0)
                amps = ig[rows, :]
                behind = jnp.where(lane == 0, 0.0, pltpu.roll(amps, 1, 1))
                y = product(bh, rows, amps - behind)
                vg[rows, :] = jnp.where(live, vg[rows, :] - y, 0.0)
            return carry

        lax.fori_loop(0, 32 // unroll, voltage_step, 0)
        if substep == SUB - 2:
            results.append(pltpu.make_async_copy(vg, vo_hbm, sems.at[1]))
            results[1].start()

    results.append(pltpu.make_async_copy(ig, io_hbm, sems.at[2]))
    results[2].start()

    def average(b, carry):
        totals = []
        for p in range(2):
            tiles = [ig[pl.ds(pl.multiple_of(b * 256 + 128 * p + 8 * i, 8), 8), :] for i in range(16)]
            while len(tiles) > 1:
                tiles = [x + y for x, y in zip(tiles[::2], tiles[1::2])]
            totals.append(tiles[0] + pltpu.roll(tiles[0], 4, 0))
        indt[pl.ds(pl.multiple_of(b * 8, 8), 8), :] = jnp.where(sub8 < 4, totals[0], totals[1]) * (1.0 / 32.0)
        return carry

    lax.fori_loop(0, 16, average, 0, unroll=4)
    ind_ref[...] = indt[...].T
    for copy in results:
        copy.wait()


def last_kernel(
    v_hbm, i_hbm, b_hbm, eg, fix_ref,
    vo_hbm, io_hbm,
    vt, it, vg, ig, bh, vo_ref, io_ref, sems, in_sems,
):
    sub8 = iota((8, 128), 0)
    lane8 = iota((8, 128), 1)
    lane = iota((128, 128), 1)
    arrivals = []
    for q in range(4):
        part = pl.ds(1024 * q, 1024)
        group = [
            pltpu.make_async_copy(src.at[part], dst.at[part], in_sems.at[m, q])
            for m, (src, dst) in enumerate(((i_hbm, ig), (b_hbm, bh), (v_hbm, vg)))
        ]
        for copy in group:
            copy.start()
        arrivals.append(group)

    for q in range(4):
        for copy in arrivals[q]:
            copy.wait()
        for u in range(8):
            g = q * 8 + u
            rows = slice(g * 128, g * 128 + 128)
            live = jnp.concatenate([lane8 < eg[8 * g : 8 * g + 8, :]] * 16, 0)
            amps = ig[rows, :]
            behind = jnp.where(lane == 0, 0.0, pltpu.roll(amps, 1, 1))
            y = product(bh, rows, amps - behind)
            vg[rows, :] = jnp.where(live, vg[rows, :] - y, 0.0)

    def ungroup(b, carry):
        rows = pl.ds(pl.multiple_of(b * 8, 8), 8)
        for src, dst in ((vg, vt), (ig, it)):
            for i in range(16):
                g0 = src[pl.ds(pl.multiple_of(b * 256 + 8 * i, 8), 8), :]
                g1 = src[pl.ds(pl.multiple_of(b * 256 + 128 + 8 * i, 8), 8), :]
                dst[2 * i, rows, :], dst[2 * i + 1, rows, :] = merge_pair(g0, g1)
        return carry

    lax.fori_loop(0, 16, ungroup, 0, unroll=2)
    copies = []
    for q in range(4):

        def turn_out(n, carry):
            c = 8 * q + n
            row = pl.ds(c, 1)
            v = vt[c].T
            i = it[c].T
            first = sub8 == 0
            second = sub8 == 1
            fix = [fix_ref[m, row, :] for m in range(5)]
            vo_ref[c] = v
            io_ref[c] = i
            vo_ref[c, 0:8, :] = v[0:8] + jnp.where(
                first, fix[0], jnp.where(second, fix[1], jnp.where(sub8 == 2, fix[2], 0.0))
            )
            io_ref[c, 0:8, :] = i[0:8] + jnp.where(first, fix[3], jnp.where(second, fix[4], 0.0))
            return carry

        lax.fori_loop(0, 8, turn_out, 0, unroll=4)
        part = pl.ds(8 * q, 8)
        for m, (src, dst) in enumerate(((vo_ref, vo_hbm), (io_ref, io_hbm))):
            copy = pltpu.make_async_copy(src.at[part], dst.at[part], sems.at[m, q])
            copy.start()
            copies.append(copy)
    for copy in copies:
        copy.wait()


def lines(voltage, current, inductance, capacitance, drive, lengths):
    big = pltpu.VMEM((32, 128, 128), F)
    flat = pltpu.VMEM((4096, 128), F)
    packed = pltpu.VMEM((4096, 256), B16)
    outside = pl.BlockSpec(memory_space=pltpu.HBM)
    inside = pl.BlockSpec(memory_space=pltpu.VMEM)
    return call(
        line_kernel,
        (shape(4096, 128), shape(4096, 128), shape(4096, 256, dtype=B16), shape(256, 128, dtype=I32),
         shape(3, 32, 128), shape(128, 128)),
        voltage, current, inductance, capacitance, drive, lengths,
        name="lines",
        in_specs=[outside] * 4 + [inside] * 2,
        out_specs=(outside, outside, outside, inside, inside, inside),
        scratch=[big, big, big, flat, flat, packed, packed, pltpu.VMEM((256, 128), F),
                 pltpu.VMEM((128, 128), F), big, big,
                 pltpu.VMEM((32, 32, 128), F), pltpu.VMEM((32, 32, 128), F),
                 pltpu.SemaphoreType.DMA((3,)), pltpu.SemaphoreType.DMA((10,))],
        limit=53,
        micros=16,
    )


def last_voltages(volts, amps, capacitance, ends_at, fix):
    big = pltpu.VMEM((32, 128, 128), F)
    flat = pltpu.VMEM((4096, 128), F)
    outside = pl.BlockSpec(memory_space=pltpu.HBM)
    inside = pl.BlockSpec(memory_space=pltpu.VMEM)
    return call(
        last_kernel,
        (shape(32, 128, 128), shape(32, 128, 128)),
        volts, amps, capacitance, ends_at, fix,
        name="last_voltages",
        in_specs=[outside] * 3 + [inside] * 2,
        out_specs=(outside, outside),
        scratch=[big, big, flat, flat, pltpu.VMEM((4096, 256), B16), big, big,
                 pltpu.SemaphoreType.DMA((2, 4)), pltpu.SemaphoreType.DMA((3, 4))],
        limit=53,
        micros=6,
    )


def junction_kernel(ends_ref, link_ref, a_ref, b_ref, ind_ref, fix_ref, indo_ref, buf):
    link = jnp.broadcast_to(link_ref[...], (8, 128))
    inflow = [
        jnp.concatenate([take(ends_ref[k, 8 * q : 8 * q + 8, :], link, 1) for q in range(4)], 0)
        for k in range(SUB)
    ]

    def apply(m_ref, x):
        buf[...] = x
        parts = [None] * 4
        for d in range(32):
            term = m_ref[d] * buf[d : d + 1, :]
            parts[d % 4] = term if parts[d % 4] is None else parts[d % 4] + term
        return (parts[0] + parts[1]) + (parts[2] + parts[3])

    f1, f2, f3 = inflow
    v1 = apply(b_ref, f1)
    i2 = apply(a_ref, v1)
    v2b = apply(b_ref, i2)
    v2a = v1 - v2b + apply(b_ref, f2)
    i3a = i2 - apply(a_ref, v2b - v2a)
    i3b = apply(a_ref, v2b)
    v3c = apply(b_ref, i3b)
    v3a = v2a - apply(b_ref, i3a - f3)
    v3b = v2b - v3c + apply(b_ref, i3a)
    sub8 = iota((8, 128), 0)
    for n, value in enumerate((v3a, v3b, v3c, i3a, i3b)):
        fix_ref[n] = value
    mean_a = jnp.sum(i3a, axis=0, keepdims=True) * (1.0 / 32.0)
    mean_b = jnp.sum(i3b, axis=0, keepdims=True) * (1.0 / 32.0)
    indo_ref[...] = ind_ref[...]
    indo_ref[0:8, :] = ind_ref[0:8, :] + jnp.where(sub8 == 0, mean_a, jnp.where(sub8 == 1, mean_b, 0.0))


def junctions(ends, link, inductance, capacitance, induced):
    return call(
        junction_kernel,
        (shape(5, 32, 128), shape(128, 128)),
        ends, link, inductance, capacitance, induced,
        name="junctions",
        scratch=[pltpu.VMEM((32, 128), F)],
        limit=3,
        micros=1,
    )


def magnetic_kernel(e_hbm, h_hbm, above_ref, ho_hbm, layer_ref, e_ref, h_ref, ho_ref, sems):
    sub = iota((8, 256), 0)
    lane = iota((8, 256), 1)

    def fetch(x):
        return (
            pltpu.make_async_copy(e_hbm.at[:, x], e_ref.at[:, x], sems.at[0, x]),
            pltpu.make_async_copy(h_hbm.at[:, x], h_ref.at[:, x], sems.at[1, x]),
        )

    def store(x):
        return pltpu.make_async_copy(ho_ref.at[:, x], ho_hbm.at[:, x], sems.at[2, x])

    for x in range(8):
        for copy in fetch(x):
            copy.start()
    fetch(0)[0].wait()

    def one_layer(x, carry):
        nx = jnp.minimum(x + 1, 7)
        last = x == 7
        for yb in range(16):
            rows = slice(8 * yb, 8 * yb + 8)
            e = [e_ref[k, x, rows, :] for k in range(3)]
            ahead = [jnp.where(last, above_ref[k, rows, :], e_ref[k + 1, nx, rows, :]) for k in range(2)]

            def diff_y(k):
                rolled = pltpu.roll(e[k], 7, 0)
                edge = e_ref[k, x, 8 * yb + 8 : 8 * yb + 9, :] if yb < 15 else jnp.zeros((1, 256), F)
                return jnp.where(sub == 7, edge, rolled) - e[k]

            def diff_z(k):
                return jnp.where(lane == 255, 0.0, pltpu.roll(e[k], 255, 1)) - e[k]

            curl = (
                diff_y(2) - diff_z(1),
                diff_z(0) - (ahead[1] - e[2]),
                (ahead[0] - e[1]) - diff_y(0),
            )
            for k in range(3):
                ho_ref[k, x, rows, :] = h_ref[k, x, rows, :] - COURANT * curl[k]
        return carry

    def layer_step(x, carry):
        @pl.when(x < 7)
        def _():
            fetch(x + 1)[0].wait()

        fetch(x)[1].wait()
        one_layer(x, carry)
        store(x).start()
        return carry

    lax.fori_loop(0, 8, layer_step, 0)
    layer_ref[...] = ho_ref[1:3, 7]
    for x in range(8):
        store(x).wait()


def magnetics(electric, magnetic, above):
    whole = pltpu.VMEM((3, 8, 128, 256), F)
    outside = pl.BlockSpec(memory_space=pltpu.HBM)
    inside = pl.BlockSpec(memory_space=pltpu.VMEM)
    return call(
        magnetic_kernel,
        (shape(3, 8, 128, 256), shape(2, 128, 256)),
        electric, magnetic, above,
        name="magnetics",
        in_specs=[outside, outside, inside],
        out_specs=(outside, inside),
        scratch=[whole, whole, whole, pltpu.SemaphoreType.DMA((3, 8))],
        limit=53,
        micros=4,
    )


def sort_columns(keys):
    sub8 = iota((8, 128), 0)
    keys = list(keys)
    size = 2
    while size <= 128:
        stride = size // 2
        while stride >= 1:
            if stride >= 8:
                gap = stride // 8
                for n in range(16):
                    if n & gap:
                        continue
                    rising = ((n * 8) & size) == 0 or size == 128
                    low = jnp.minimum(keys[n], keys[n + gap])
                    high = jnp.maximum(keys[n], keys[n + gap])
                    keys[n], keys[n + gap] = (low, high) if rising else (high, low)
            else:
                partner = sub8 ^ stride
                first = (sub8 & stride) == 0
                for n in range(16):
                    other = take(keys[n], partner, 0)
                    if size >= 8:
                        rising = ((n * 8) & size) == 0 or size == 128
                        want_low = first if rising else ~first
                    else:
                        want_low = ((sub8 & size) == 0) == first
                    keys[n] = jnp.where(want_low, jnp.minimum(keys[n], other), jnp.maximum(keys[n], other))
            stride //= 2
        size *= 2
    return keys


def search_kernel(idx_ref, cell_ref, perm_ref, pos_ref):
    sub8 = iota((8, 128), 0)
    lane8 = iota((8, 128), 1)
    keys = []
    for n in range(16):
        owner = sub8 + 8 * n
        cell = idx_ref[8 * n : 8 * n + 8, :]
        keys.append(((owner & 1) * 1024 + cell) * 128 + owner)
    keys = jnp.concatenate(sort_columns(keys), 0).T
    cell_ref[...] = keys >> 7
    perm_ref[...] = keys & 127

    def spread(n, carry):
        rows = pl.ds(pl.multiple_of(n * 8, 8), 8)
        cell = cell_ref[rows, :]
        for h in range(2):
            fence = {
                p: take(cell, jnp.full((8, 128), 64 * h + p, I32), 1)
                for p in (0, 8, 16, 24, 32, 40, 48, 56)
            }
            chains = []
            for x in range(8):
                target = lane8 + (h * 1024 + x * 128)
                up = fence[32] <= target
                pos = jnp.where(up, 64 * h + 32, 64 * h)
                cur = jnp.where(up, fence[32], fence[0])
                probe = jnp.where(up, fence[48], fence[16])
                up2 = probe <= target
                pos = jnp.where(up2, pos + 16, pos)
                cur = jnp.where(up2, probe, cur)
                probe = jnp.where(
                    up,
                    jnp.where(up2, fence[56], fence[40]),
                    jnp.where(up2, fence[24], fence[8]),
                )
                hit = probe <= target
                chains.append((target, jnp.where(hit, pos + 8, pos), jnp.where(hit, probe, cur)))
            for step in (4, 2, 1):
                probes = [take(cell, pos + step, 1) for _, pos, _ in chains]
                hits = [probe <= chain[0] for probe, chain in zip(probes, chains)]
                chains = [
                    (target, jnp.where(hit, pos + step, pos), jnp.where(hit, probe, cur))
                    for (target, pos, cur), probe, hit in zip(chains, probes, hits)
                ]
            for x, (target, pos, cur) in enumerate(chains):
                pos_ref[h, x, rows, :] = jnp.where(cur == target, pos, -1)
        return carry

    lax.fori_loop(0, 16, spread, 0)


def search(cells):
    return call(
        search_kernel,
        (shape(128, 128, dtype=I32), shape(128, 128, dtype=I32), shape(2, 8, 128, 128, dtype=I32)),
        cells,
        name="search",
        limit=4,
        micros=4,
    )


def electric_kernel(
    e_hbm, h_hbm, below_ref, sigma_hbm, ind_ref, tan_ref, cell_s, perm_s, pos_hbm,
    eo_hbm, val_s, plane_s, plane_t, eo_ref, e_ref, h_ref, sigma_ref, pos_ref, sems, in_sems,
):
    def fetch(x):
        return (
            pltpu.make_async_copy(pos_hbm.at[:, x], pos_ref.at[:, x], in_sems.at[0, x]),
            pltpu.make_async_copy(h_hbm.at[:, x], h_ref.at[:, x], in_sems.at[1, x]),
            pltpu.make_async_copy(e_hbm.at[:, x], e_ref.at[:, x], in_sems.at[2, x]),
            pltpu.make_async_copy(sigma_hbm.at[x], sigma_ref.at[x], in_sems.at[3, x]),
        )

    for x in range(8):
        for copy in fetch(x):
            copy.start()
    for k in range(3):
        val_s[k] = (tan_ref[k] * ind_ref[...]).T
    for start in range(0, 16, 8):
        spans = [slice(8 * n, 8 * n + 8) for n in range(start, start + 8)]
        cells = [cell_s[rows, :] for rows in spans]
        val = [[take(val_s[k, rows, :], perm_s[rows, :], 1) for k in range(3)] for rows in spans]
        for gap in (1, 2, 4, 8, 16, 32):
            same = [pltpu.roll(cell, gap, 1) == cell for cell in cells]
            moved = [[pltpu.roll(v, gap, 1) for v in row] for row in val]
            val = [
                [v + jnp.where(hit, w, 0.0) for v, w in zip(row, shifted)]
                for row, shifted, hit in zip(val, moved, same)
            ]
        for rows, row in zip(spans, val):
            for k in range(3):
                val_s[k, rows, :] = row[k]

    sub = iota((8, 256), 0)
    lane = iota((8, 256), 1)

    def spread_layer(x, plane_s):
        for h in range(2):
            tiles = [[], [], []]
            for n in range(16):
                pos = pos_ref[h, x, 8 * n : 8 * n + 8, :]
                spot = pos & 127
                for k in range(3):
                    picked = take(val_s[k, 8 * n : 8 * n + 8, :], spot, 1)
                    tiles[k].append(jnp.where(pos >= 0, picked, 0.0))
            for k in range(3):
                plane_s[k, :, 128 * h : 128 * h + 128] = jnp.concatenate(tiles[k], 0).T

    def update_layer(x, plane_s):
        px = jnp.maximum(x - 1, 0)
        first = x == 0
        for yb in range(16):
            rows = slice(8 * yb, 8 * yb + 8)
            m = [h_ref[k, x, rows, :] for k in range(3)]
            behind = [jnp.where(first, below_ref[k, rows, :], h_ref[k + 1, px, rows, :]) for k in range(2)]

            def diff_y(k):
                rolled = pltpu.roll(m[k], 1, 0)
                edge = h_ref[k, x, 8 * yb - 1 : 8 * yb, :] if yb > 0 else jnp.zeros((1, 256), F)
                return m[k] - jnp.where(sub == 0, edge, rolled)

            def diff_z(k):
                return m[k] - jnp.where(lane == 0, 0.0, pltpu.roll(m[k], 1, 1))

            curl = (
                diff_y(2) - diff_z(1),
                diff_z(0) - (m[2] - behind[1]),
                (m[1] - behind[0]) - diff_y(0),
            )
            sigma = sigma_ref[x, rows, :]
            inverse = 1.0 / (1.0 + sigma)
            keep = (1.0 - sigma) * inverse
            push = COURANT * inverse
            for k in range(3):
                eo_ref[k, x, rows, :] = keep * e_ref[k, x, rows, :] + push * (curl[k] - plane_s[k, rows, :])
        pltpu.make_async_copy(eo_ref.at[:, x], eo_hbm.at[:, x], sems.at[x]).start()

    def arrive(x, which):
        for copy in fetch(x)[which]:
            copy.wait()

    early, late = slice(0, 1), slice(1, 4)
    arrive(0, early)
    spread_layer(0, plane_s)

    def two_layers(n, carry):
        x = 2 * n
        arrive(x + 1, early)
        arrive(x, late)
        spread_layer(x + 1, plane_t)
        update_layer(x, plane_s)

        @pl.when(n < 3)
        def _():
            arrive(x + 2, early)

        arrive(x + 1, late)
        spread_layer(jnp.minimum(x + 2, 7), plane_s)
        update_layer(x + 1, plane_t)
        return carry

    lax.fori_loop(0, 4, two_layers, 0)
    for x in range(8):
        pltpu.make_async_copy(eo_ref.at[:, x], eo_hbm.at[:, x], sems.at[x]).wait()


def electrics(electric, magnetic_new, below, conductivity, induced, tangent, found):
    whole = pltpu.VMEM((3, 8, 128, 256), F)
    outside = pl.BlockSpec(memory_space=pltpu.HBM)
    inside = pl.BlockSpec(memory_space=pltpu.VMEM)
    return call(
        electric_kernel,
        shape(3, 8, 128, 256),
        electric, magnetic_new, below, conductivity, induced, tangent, *found,
        name="electrics",
        in_specs=[outside, outside, inside, outside, inside, inside, inside, inside, outside],
        out_specs=outside,
        scratch=[
            pltpu.VMEM((3, 128, 128), F),
            pltpu.VMEM((3, 128, 256), F),
            pltpu.VMEM((3, 128, 256), F),
            whole, whole, whole,
            pltpu.VMEM((8, 128, 256), F),
            pltpu.VMEM((2, 8, 128, 128), I32),
            pltpu.SemaphoreType.DMA((8,)),
            pltpu.SemaphoreType.DMA((4, 8)),
        ],
        limit=53,
        micros=6,
    )


BOTH = ("slab", "cable")


def along(x, axis, by):
    peers = lax.axis_size(axis)
    return lax.ppermute(x, axis, [(i, i + by) for i in range(peers) if 0 <= i + by < peers])


def around(x, axis):
    peers = lax.axis_size(axis)
    return lax.ppermute(x, axis, [(i, (i + 1) % peers) for i in range(peers)])


def exchange(x):
    return lax.all_to_all(x, BOTH, split_axis=0, concat_axis=0, tiled=True)


def local(
    electric, magnetic, conductivity, voltage, current, inverse_inductance,
    inverse_capacitance, tangent, sample_cell, tube_length, junction_link,
):
    cells = sample_cell.reshape(128, 128)
    steer = tangent.reshape(3, 128, 128)
    drive_local, layer = samples(electric, cells, steer)
    above = along(layer, BOTH, -1)
    drive = exchange(drive_local)
    magnetic_new, layer = magnetics(electric, magnetic, above)
    drive, layer = lax.optimization_barrier((drive, layer))
    below = along(layer, BOTH, 1)
    *state, ends, induced = lines(
        voltage, current, inverse_inductance, inverse_capacitance, drive, tube_length.reshape(1, 128)
    )
    ends, cells = lax.optimization_barrier((ends, cells))
    ends = around(ends, "cable")
    found = search(cells)
    fix, induced = junctions(
        ends, junction_link.reshape(1, 128), inverse_inductance, inverse_capacitance, induced
    )
    induced, found = lax.optimization_barrier((induced, found))
    induced_local = exchange(induced)
    volts, amps = last_voltages(*state, fix)
    electric_new = electrics(electric, magnetic_new, below, conductivity, induced_local, steer, found)
    return electric_new, magnetic_new, volts, amps


def solution(mesh):
    grid = P(None, BOTH, None, None)
    tubes = P(None, None, BOTH)
    return jax.shard_map(
        local,
        mesh=mesh,
        in_specs=(
            grid, grid, P(BOTH, None, None), tubes, tubes, tubes, tubes,
            P(None, BOTH, None), P(BOTH, None), P(BOTH), P(BOTH),
        ),
        out_specs=(grid, grid, tubes, tubes),
        check_vma=False,
    )
```

```python
import jax
import jax.numpy as jnp
from jax import lax
from jax.experimental import pallas as pl
from jax.experimental.pallas import tpu as pltpu
from jax.sharding import PartitionSpec as P

F = jnp.float32
B16 = jnp.bfloat16
I32 = jnp.int32
SUB = 3
COURANT = 0.5
MB = 2**20


def take(x, index, axis):
    return jnp.take_along_axis(x, index, axis=axis, mode="promise_in_bounds")


def iota(shape, axis):
    return lax.broadcasted_iota(I32, shape, axis)


def call(body, out, *ins, name, scratch=(), limit=40, in_specs=None, aliases=None, out_specs=None, micros=None, grid=()):
    kw = {}
    if in_specs is not None:
        kw["in_specs"] = in_specs
    if out_specs is not None:
        kw["out_specs"] = out_specs
    return pl.pallas_call(
        body,
        out_shape=out,
        grid=grid,
        scratch_shapes=list(scratch),
        input_output_aliases=aliases or {},
        compiler_params=pltpu.CompilerParams(vmem_limit_bytes=limit * MB),
        cost_estimate=pl.CostEstimate(flops=0, bytes_accessed=int(micros * 3.69e6), transcendentals=0) if micros else None,
        name=name,
        **kw,
    )(*ins)


def shape(*dims, dtype=F):
    return jax.ShapeDtypeStruct(dims, dtype)


def gather_kernel(e_hbm, idx_hbm, tan_hbm, drive_ref, layer_ref, e_ref, idx_ref, tan_ref, sems):
    copies = [pltpu.make_async_copy(e_hbm.at[:, x], e_ref.at[:, x], sems.at[x]) for x in range(8)]
    idx_copy = pltpu.make_async_copy(idx_hbm, idx_ref, sems.at[8])
    tan_copy = pltpu.make_async_copy(tan_hbm, tan_ref, sems.at[9])
    idx_copy.start()
    for copy in copies:
        copy.start()
    tan_copy.start()
    idx_copy.wait()
    for h in range(2):
        lanes = pl.ds(h * 128, 128)
        rows = pl.ds(h, 64, stride=2)
        idx = idx_ref[rows, :]
        idx = [idx[8 * g : 8 * g + 8] for g in range(8)]
        low = [i & 7 for i in idx]
        high = [i >> 3 for i in idx]
        acc = (jnp.zeros((8, 128), F),) * 24
        for x in range(8):
            if h == 0:
                copies[x].wait()

            def step(yb, acc):
                acc = list(acc)
                yrows = pl.ds(pl.multiple_of(yb * 8, 8), 8)
                src = [e_ref[k, x, yrows, lanes] for k in range(3)]
                for g in range(8):
                    hit = high[g] == yb + 16 * x
                    for k in range(3):
                        acc[g * 3 + k] = jnp.where(hit, take(src[k], low[g], 0), acc[g * 3 + k])
                return tuple(acc)

            acc = lax.fori_loop(0, 16, step, acc, unroll=4)
        if h == 0:
            tan_copy.wait()
            layer_ref[...] = e_ref[1:3, 0]
        picked = [jnp.concatenate([acc[g * 3 + k] for g in range(8)], 0) for k in range(3)]
        steer = [tan_ref[k, rows, :] for k in range(3)]
        drive_ref[rows, :] = steer[0] * picked[0] + steer[1] * picked[1] + steer[2] * picked[2]


def samples(electric, cells, steer):
    return call(
        gather_kernel,
        (shape(128, 128), shape(2, 128, 256)),
        electric, cells, steer,
        name="samples",
        in_specs=[pl.BlockSpec(memory_space=pltpu.HBM)] * 3,
        scratch=[
            pltpu.VMEM((3, 8, 128, 256), F),
            pltpu.VMEM((128, 128), I32),
            pltpu.VMEM((3, 128, 128), F),
            pltpu.SemaphoreType.DMA((10,)),
        ],
        limit=58,
        micros=4,
    )


def merge_pair(x, y):
    low = iota((8, 128), 0) < 4
    return jnp.where(low, x, pltpu.roll(y, 4, 0)), jnp.where(low, pltpu.roll(x, 4, 0), y)


def split_parts(x):
    high = x.astype(B16)
    return high, (x - high.astype(F)).astype(B16)


def product(m_ref, rows, x):
    high, low = split_parts(x)
    rhs = jnp.concatenate([high, low], 1)
    rhs = jnp.concatenate([rhs, rhs], 0)
    y = jnp.dot(m_ref[rows, :], rhs, preferred_element_type=F)
    return y[:, :128] + y[:, 128:]


def line_kernel(
    v_hbm, i_hbm, a_hbm, b_hbm, drive_ref, len_ref,
    vo_hbm, io_hbm, bo_hbm, eg, ends_ref, ind_ref,
    vt, it, at, vg, ig, ah, bh, dg, indt, v_ref, i_ref, a_ref, b_ref, sems, in_sems,
):
    matrices = [
        pltpu.make_async_copy(src, dst, in_sems.at[8 + m])
        for m, (src, dst) in enumerate(((a_hbm, a_ref), (b_hbm, b_ref)))
    ]
    for copy in matrices:
        copy.start()
    arrivals = []
    for q in range(4):
        part = pl.ds(8 * q, 8)
        pair = [
            pltpu.make_async_copy(src.at[part], dst.at[part], in_sems.at[2 * q + m])
            for m, (src, dst) in enumerate(((v_hbm, v_ref), (i_hbm, i_ref)))
        ]
        for copy in pair:
            copy.start()
        arrivals.append(pair)
    sub8 = iota((8, 128), 0)
    lane8 = iota((8, 128), 1)
    lane = iota((128, 128), 1)


    spread = [(sub8 >> 2) + 2 * j for j in range(4)]
    own = (sub8 & 3) == (lane8 & 3)
    for m_ref, dst, arrival in ((a_ref, ah, matrices[0]), (b_ref, bh, matrices[1])):
        arrival.wait()

        def expand(c, carry):
            tiles = []
            for q in range(4):
                tile = m_ref[c, 8 * q : 8 * q + 8, :]
                for j in range(4):
                    tiles.append(jnp.where(own, take(tile, spread[j], 0), 0.0))
            at[c] = jnp.concatenate(tiles, 0).T
            return carry

        lax.fori_loop(0, 32, expand, 0, unroll=4)

        def pack(b, carry):
            rows = pl.ds(pl.multiple_of(b * 8, 8), 8)
            first, second = [], []
            for i in range(16):
                g0, g1 = merge_pair(at[2 * i, rows, :], at[2 * i + 1, rows, :])
                first.append(g0)
                second.append(g1)
            for p, tiles in enumerate((first, second)):
                high, low = split_parts(jnp.concatenate(tiles, 0))
                out_rows = pl.ds(pl.multiple_of(b * 256 + p * 128, 128), 128)
                dst[out_rows, 0:128] = high
                dst[out_rows, 128:256] = low
            return carry

        lax.fori_loop(0, 16, pack, 0, unroll=2)

    results = [pltpu.make_async_copy(bh, bo_hbm, sems.at[0])]
    results[0].start()

    def turn_in(c, carry):
        vt[c] = v_ref[c].T
        it[c] = i_ref[c].T
        return carry

    for q in range(4):
        for copy in arrivals[q]:
            copy.wait()
        lax.fori_loop(8 * q, 8 * q + 8, turn_in, 0, unroll=4)
    def regroup(b, carry):
        rows = pl.ds(pl.multiple_of(b * 8, 8), 8)
        for src, dst in ((vt, vg), (it, ig)):
            for i in range(16):
                g0, g1 = merge_pair(src[2 * i, rows, :], src[2 * i + 1, rows, :])
                dst[pl.ds(pl.multiple_of(b * 256 + 8 * i, 8), 8), :] = g0
                dst[pl.ds(pl.multiple_of(b * 256 + 128 + 8 * i, 8), 8), :] = g1
        return carry

    lax.fori_loop(0, 16, regroup, 0, unroll=2)

    at[0] = drive_ref[...].T
    at[1] = jnp.broadcast_to(len_ref[...].astype(F), (128, 128)).T
    for b in range(16):
        rows = slice(8 * b, 8 * b + 8)
        for p, value in enumerate(merge_pair(at[0, rows, :], at[0, rows, :])):
            dg[16 * b + 8 * p : 16 * b + 8 * p + 8, :] = value
        for p, value in enumerate(merge_pair(at[1, rows, :], at[1, rows, :])):
            eg[16 * b + 8 * p : 16 * b + 8 * p + 8, :] = value.astype(I32)

    unroll = 16
    for substep in range(SUB):

        def current_step(n, acc):
            for u in range(unroll):
                g = n * unroll + u
                rows = pl.ds(pl.multiple_of(g * 128, 128), 128)
                small = pl.ds(pl.multiple_of(g * 8, 8), 8)
                length = eg[small, :]
                live = jnp.concatenate([lane8 < length] * 16, 0)
                drive = jnp.concatenate([dg[small, :]] * 16, 0)
                volts = vg[rows, :]
                ahead = jnp.where(lane == 127, 0.0, pltpu.roll(volts, 127, 1))
                y = product(ah, rows, ahead - volts - drive)
                amps = jnp.where(live, ig[rows, :] - y, 0.0)
                ig[rows, :] = amps
                spot = lane8 == 4 * g + (sub8 & 3)
                acc = tuple(
                    jnp.where(spot, take(amps[8 * i : 8 * i + 8], length - 1, 1), acc[i])
                    for i in range(16)
                )
            return acc

        acc = lax.fori_loop(0, 32 // unroll, current_step, (jnp.zeros((8, 128), F),) * 16)
        pick = (sub8 & 1) * 4 + (lane8 & 3)
        for q in range(4):
            out = take(acc[4 * q], pick, 0)
            for i in range(1, 4):
                out = jnp.where((sub8 >> 1) == i, take(acc[4 * q + i], pick, 0), out)
            ends_ref[substep, 8 * q : 8 * q + 8, :] = out

        if substep == SUB - 1:
            break

        def voltage_step(n, carry):
            for u in range(unroll):
                g = n * unroll + u
                rows = pl.ds(pl.multiple_of(g * 128, 128), 128)
                small = pl.ds(pl.multiple_of(g * 8, 8), 8)
                live = jnp.concatenate([lane8 < eg[small, :]] * 16, 0)
                amps = ig[rows, :]
                behind = jnp.where(lane == 0, 0.0, pltpu.roll(amps, 1, 1))
                y = product(bh, rows, amps - behind)
                vg[rows, :] = jnp.where(live, vg[rows, :] - y, 0.0)
            return carry

        lax.fori_loop(0, 32 // unroll, voltage_step, 0)
        if substep == SUB - 2:
            results.append(pltpu.make_async_copy(vg, vo_hbm, sems.at[1]))
            results[1].start()

    results.append(pltpu.make_async_copy(ig, io_hbm, sems.at[2]))
    results[2].start()

    def average(b, carry):
        totals = []
        for p in range(2):
            tiles = [ig[pl.ds(pl.multiple_of(b * 256 + 128 * p + 8 * i, 8), 8), :] for i in range(16)]
            while len(tiles) > 1:
                tiles = [x + y for x, y in zip(tiles[::2], tiles[1::2])]
            totals.append(tiles[0] + pltpu.roll(tiles[0], 4, 0))
        indt[pl.ds(pl.multiple_of(b * 8, 8), 8), :] = jnp.where(sub8 < 4, totals[0], totals[1]) * (1.0 / 32.0)
        return carry

    lax.fori_loop(0, 16, average, 0, unroll=4)
    ind_ref[...] = indt[...].T
    for copy in results:
        copy.wait()


def last_kernel(
    v_hbm, i_hbm, b_hbm, eg, fix_ref,
    vo_hbm, io_hbm,
    vt, it, vg, ig, bh, vo_ref, io_ref, sems, in_sems,
):
    sub8 = iota((8, 128), 0)
    lane8 = iota((8, 128), 1)
    lane = iota((128, 128), 1)
    arrivals = []
    for q in range(4):
        part = pl.ds(1024 * q, 1024)
        group = [
            pltpu.make_async_copy(src.at[part], dst.at[part], in_sems.at[m, q])
            for m, (src, dst) in enumerate(((i_hbm, ig), (b_hbm, bh), (v_hbm, vg)))
        ]
        for copy in group:
            copy.start()
        arrivals.append(group)

    for q in range(4):
        for copy in arrivals[q]:
            copy.wait()
        for u in range(8):
            g = q * 8 + u
            rows = slice(g * 128, g * 128 + 128)
            live = jnp.concatenate([lane8 < eg[8 * g : 8 * g + 8, :]] * 16, 0)
            amps = ig[rows, :]
            behind = jnp.where(lane == 0, 0.0, pltpu.roll(amps, 1, 1))
            y = product(bh, rows, amps - behind)
            vg[rows, :] = jnp.where(live, vg[rows, :] - y, 0.0)

    def ungroup(b, carry):
        rows = pl.ds(pl.multiple_of(b * 8, 8), 8)
        for src, dst in ((vg, vt), (ig, it)):
            for i in range(16):
                g0 = src[pl.ds(pl.multiple_of(b * 256 + 8 * i, 8), 8), :]
                g1 = src[pl.ds(pl.multiple_of(b * 256 + 128 + 8 * i, 8), 8), :]
                dst[2 * i, rows, :], dst[2 * i + 1, rows, :] = merge_pair(g0, g1)
        return carry

    lax.fori_loop(0, 16, ungroup, 0, unroll=2)
    copies = []
    for q in range(4):

        def turn_out(n, carry):
            c = 8 * q + n
            row = pl.ds(c, 1)
            v = vt[c].T
            i = it[c].T
            first = sub8 == 0
            second = sub8 == 1
            fix = [fix_ref[m, row, :] for m in range(5)]
            vo_ref[c] = v
            io_ref[c] = i
            vo_ref[c, 0:8, :] = v[0:8] + jnp.where(
                first, fix[0], jnp.where(second, fix[1], jnp.where(sub8 == 2, fix[2], 0.0))
            )
            io_ref[c, 0:8, :] = i[0:8] + jnp.where(first, fix[3], jnp.where(second, fix[4], 0.0))
            return carry

        lax.fori_loop(0, 8, turn_out, 0, unroll=4)
        part = pl.ds(8 * q, 8)
        for m, (src, dst) in enumerate(((vo_ref, vo_hbm), (io_ref, io_hbm))):
            copy = pltpu.make_async_copy(src.at[part], dst.at[part], sems.at[m, q])
            copy.start()
            copies.append(copy)
    for copy in copies:
        copy.wait()


def lines(voltage, current, inductance, capacitance, drive, lengths):
    big = pltpu.VMEM((32, 128, 128), F)
    flat = pltpu.VMEM((4096, 128), F)
    packed = pltpu.VMEM((4096, 256), B16)
    outside = pl.BlockSpec(memory_space=pltpu.HBM)
    inside = pl.BlockSpec(memory_space=pltpu.VMEM)
    return call(
        line_kernel,
        (shape(4096, 128), shape(4096, 128), shape(4096, 256, dtype=B16), shape(256, 128, dtype=I32),
         shape(3, 32, 128), shape(128, 128)),
        voltage, current, inductance, capacitance, drive, lengths,
        name="lines",
        in_specs=[outside] * 4 + [inside] * 2,
        out_specs=(outside, outside, outside, inside, inside, inside),
        scratch=[big, big, big, flat, flat, packed, packed, pltpu.VMEM((256, 128), F),
                 pltpu.VMEM((128, 128), F), big, big,
                 pltpu.VMEM((32, 32, 128), F), pltpu.VMEM((32, 32, 128), F),
                 pltpu.SemaphoreType.DMA((3,)), pltpu.SemaphoreType.DMA((10,))],
        limit=53,
        micros=16,
    )


def last_voltages(volts, amps, capacitance, ends_at, fix):
    big = pltpu.VMEM((32, 128, 128), F)
    flat = pltpu.VMEM((4096, 128), F)
    outside = pl.BlockSpec(memory_space=pltpu.HBM)
    inside = pl.BlockSpec(memory_space=pltpu.VMEM)
    return call(
        last_kernel,
        (shape(32, 128, 128), shape(32, 128, 128)),
        volts, amps, capacitance, ends_at, fix,
        name="last_voltages",
        in_specs=[outside] * 3 + [inside] * 2,
        out_specs=(outside, outside),
        scratch=[big, big, flat, flat, pltpu.VMEM((4096, 256), B16), big, big,
                 pltpu.SemaphoreType.DMA((2, 4)), pltpu.SemaphoreType.DMA((3, 4))],
        limit=53,
        micros=6,
    )


def junction_kernel(ends_ref, link_ref, a_ref, b_ref, ind_ref, fix_ref, indo_ref, buf):
    link = jnp.broadcast_to(link_ref[...], (8, 128))
    inflow = [
        jnp.concatenate([take(ends_ref[k, 8 * q : 8 * q + 8, :], link, 1) for q in range(4)], 0)
        for k in range(SUB)
    ]

    def apply(m_ref, x):
        buf[...] = x
        parts = [None] * 4
        for d in range(32):
            term = m_ref[d] * buf[d : d + 1, :]
            parts[d % 4] = term if parts[d % 4] is None else parts[d % 4] + term
        return (parts[0] + parts[1]) + (parts[2] + parts[3])

    f1, f2, f3 = inflow
    v1 = apply(b_ref, f1)
    i2 = apply(a_ref, v1)
    v2b = apply(b_ref, i2)
    v2a = v1 - v2b + apply(b_ref, f2)
    i3a = i2 - apply(a_ref, v2b - v2a)
    i3b = apply(a_ref, v2b)
    v3c = apply(b_ref, i3b)
    v3a = v2a - apply(b_ref, i3a - f3)
    v3b = v2b - v3c + apply(b_ref, i3a)
    sub8 = iota((8, 128), 0)
    for n, value in enumerate((v3a, v3b, v3c, i3a, i3b)):
        fix_ref[n] = value
    mean_a = jnp.sum(i3a, axis=0, keepdims=True) * (1.0 / 32.0)
    mean_b = jnp.sum(i3b, axis=0, keepdims=True) * (1.0 / 32.0)
    indo_ref[...] = ind_ref[...]
    indo_ref[0:8, :] = ind_ref[0:8, :] + jnp.where(sub8 == 0, mean_a, jnp.where(sub8 == 1, mean_b, 0.0))


def junctions(ends, link, inductance, capacitance, induced):
    return call(
        junction_kernel,
        (shape(5, 32, 128), shape(128, 128)),
        ends, link, inductance, capacitance, induced,
        name="junctions",
        scratch=[pltpu.VMEM((32, 128), F)],
        limit=3,
        micros=1,
    )


def magnetic_kernel(e_hbm, h_hbm, above_ref, ho_hbm, layer_ref, e_ref, h_ref, ho_ref, sems):
    sub = iota((8, 256), 0)
    lane = iota((8, 256), 1)

    def fetch(x):
        return (
            pltpu.make_async_copy(e_hbm.at[:, x], e_ref.at[:, x], sems.at[0, x]),
            pltpu.make_async_copy(h_hbm.at[:, x], h_ref.at[:, x], sems.at[1, x]),
        )

    def store(x):
        return pltpu.make_async_copy(ho_ref.at[:, x], ho_hbm.at[:, x], sems.at[2, x])

    for x in range(8):
        for copy in fetch(x):
            copy.start()
    fetch(0)[0].wait()

    def one_layer(x, carry):
        nx = jnp.minimum(x + 1, 7)
        last = x == 7
        for yb in range(16):
            rows = slice(8 * yb, 8 * yb + 8)
            e = [e_ref[k, x, rows, :] for k in range(3)]
            ahead = [jnp.where(last, above_ref[k, rows, :], e_ref[k + 1, nx, rows, :]) for k in range(2)]

            def diff_y(k):
                rolled = pltpu.roll(e[k], 7, 0)
                edge = e_ref[k, x, 8 * yb + 8 : 8 * yb + 9, :] if yb < 15 else jnp.zeros((1, 256), F)
                return jnp.where(sub == 7, edge, rolled) - e[k]

            def diff_z(k):
                return jnp.where(lane == 255, 0.0, pltpu.roll(e[k], 255, 1)) - e[k]

            curl = (
                diff_y(2) - diff_z(1),
                diff_z(0) - (ahead[1] - e[2]),
                (ahead[0] - e[1]) - diff_y(0),
            )
            for k in range(3):
                ho_ref[k, x, rows, :] = h_ref[k, x, rows, :] - COURANT * curl[k]
        return carry

    def layer_step(x, carry):
        @pl.when(x < 7)
        def _():
            fetch(x + 1)[0].wait()

        fetch(x)[1].wait()
        one_layer(x, carry)
        store(x).start()
        return carry

    lax.fori_loop(0, 8, layer_step, 0)
    layer_ref[...] = ho_ref[1:3, 7]
    for x in range(8):
        store(x).wait()


def magnetics(electric, magnetic, above):
    whole = pltpu.VMEM((3, 8, 128, 256), F)
    outside = pl.BlockSpec(memory_space=pltpu.HBM)
    inside = pl.BlockSpec(memory_space=pltpu.VMEM)
    return call(
        magnetic_kernel,
        (shape(3, 8, 128, 256), shape(2, 128, 256)),
        electric, magnetic, above,
        name="magnetics",
        in_specs=[outside, outside, inside],
        out_specs=(outside, inside),
        scratch=[whole, whole, whole, pltpu.SemaphoreType.DMA((3, 8))],
        limit=53,
        micros=4,
    )


def sort_columns(keys):
    sub8 = iota((8, 128), 0)
    keys = list(keys)
    size = 2
    while size <= 128:
        stride = size // 2
        while stride >= 1:
            if stride >= 8:
                gap = stride // 8
                for n in range(16):
                    if n & gap:
                        continue
                    rising = ((n * 8) & size) == 0 or size == 128
                    low = jnp.minimum(keys[n], keys[n + gap])
                    high = jnp.maximum(keys[n], keys[n + gap])
                    keys[n], keys[n + gap] = (low, high) if rising else (high, low)
            else:
                partner = sub8 ^ stride
                first = (sub8 & stride) == 0
                for n in range(16):
                    other = take(keys[n], partner, 0)
                    if size >= 8:
                        rising = ((n * 8) & size) == 0 or size == 128
                        want_low = first if rising else ~first
                    else:
                        want_low = ((sub8 & size) == 0) == first
                    keys[n] = jnp.where(want_low, jnp.minimum(keys[n], other), jnp.maximum(keys[n], other))
            stride //= 2
        size *= 2
    return keys


def sort_cells(idx_ref, cell_ref, perm_ref):
    sub8 = iota((8, 128), 0)
    keys = []
    for n in range(16):
        owner = sub8 + 8 * n
        cell = idx_ref[8 * n : 8 * n + 8, :]
        keys.append(((owner & 1) * 1024 + cell) * 128 + owner)
    keys = jnp.concatenate(sort_columns(keys), 0).T
    cell_ref[...] = keys >> 7
    perm_ref[...] = keys & 127


def find_cells(cell_ref, pos_ref, start):
    lane8 = iota((8, 128), 1)

    def spread(n, carry):
        rows = pl.ds(pl.multiple_of(n * 8, 8), 8)
        cell = cell_ref[pl.ds(pl.multiple_of(start + n * 8, 8), 8), :]
        for h in range(2):
            fence = {
                p: take(cell, jnp.full((8, 128), 64 * h + p, I32), 1)
                for p in (0, 8, 16, 24, 32, 40, 48, 56)
            }
            chains = []
            for x in range(8):
                target = lane8 + (h * 1024 + x * 128)
                up = fence[32] <= target
                pos = jnp.where(up, 64 * h + 32, 64 * h)
                cur = jnp.where(up, fence[32], fence[0])
                probe = jnp.where(up, fence[48], fence[16])
                up2 = probe <= target
                pos = jnp.where(up2, pos + 16, pos)
                cur = jnp.where(up2, probe, cur)
                probe = jnp.where(
                    up,
                    jnp.where(up2, fence[56], fence[40]),
                    jnp.where(up2, fence[24], fence[8]),
                )
                hit = probe <= target
                chains.append((target, jnp.where(hit, pos + 8, pos), jnp.where(hit, probe, cur)))
            for step in (4, 2, 1):
                probes = [take(cell, pos + step, 1) for _, pos, _ in chains]
                hits = [probe <= chain[0] for probe, chain in zip(probes, chains)]
                chains = [
                    (target, jnp.where(hit, pos + step, pos), jnp.where(hit, probe, cur))
                    for (target, pos, cur), probe, hit in zip(chains, probes, hits)
                ]
            for x, (target, pos, cur) in enumerate(chains):
                pos_ref[h, x, rows, :] = jnp.where(cur == target, pos, -1)
        return carry

    lax.fori_loop(0, 8, spread, 0)


def first_search_kernel(idx_ref, cell_ref, perm_ref, pos_ref):
    sort_cells(idx_ref, cell_ref, perm_ref)
    find_cells(cell_ref, pos_ref, 0)


def second_search_kernel(cell_ref, pos_ref):
    find_cells(cell_ref, pos_ref, 64)


HALF = (2, 8, 64, 128)


def first_search(cells):
    return call(
        first_search_kernel,
        (shape(128, 128, dtype=I32), shape(128, 128, dtype=I32), shape(*HALF, dtype=I32)),
        cells,
        name="first_search",
        limit=53,
        micros=3,
    )


def second_search(cell):
    return call(second_search_kernel, shape(*HALF, dtype=I32), cell, name="second_search", limit=53, micros=3)


def search(cells):
    cell, perm, pos = first_search(cells)
    return cell, perm, pos, second_search(cell)


def electric_kernel(
    e_hbm, h_hbm, below_ref, sigma_hbm, ind_ref, tan_ref, cell_s, perm_s, pos_a, pos_b,
    eo_hbm, val_s, plane_s, plane_t, eo_ref, e_ref, h_ref, sigma_ref, pos_ref, sems, in_sems,
):
    def fetch(x):
        return (
            pltpu.make_async_copy(pos_a.at[:, x], pos_ref.at[0, :, x], in_sems.at[0, x]),
            pltpu.make_async_copy(pos_b.at[:, x], pos_ref.at[1, :, x], in_sems.at[4, x]),
            pltpu.make_async_copy(h_hbm.at[:, x], h_ref.at[:, x], in_sems.at[1, x]),
            pltpu.make_async_copy(e_hbm.at[:, x], e_ref.at[:, x], in_sems.at[2, x]),
            pltpu.make_async_copy(sigma_hbm.at[x], sigma_ref.at[x], in_sems.at[3, x]),
        )

    for x in range(8):
        for copy in fetch(x):
            copy.start()
    for k in range(3):
        val_s[k] = (tan_ref[k] * ind_ref[...]).T
    for start in range(0, 16, 8):
        spans = [slice(8 * n, 8 * n + 8) for n in range(start, start + 8)]
        cells = [cell_s[rows, :] for rows in spans]
        val = [[take(val_s[k, rows, :], perm_s[rows, :], 1) for k in range(3)] for rows in spans]
        for gap in (1, 2, 4, 8, 16, 32):
            same = [pltpu.roll(cell, gap, 1) == cell for cell in cells]
            moved = [[pltpu.roll(v, gap, 1) for v in row] for row in val]
            val = [
                [v + jnp.where(hit, w, 0.0) for v, w in zip(row, shifted)]
                for row, shifted, hit in zip(val, moved, same)
            ]
        for rows, row in zip(spans, val):
            for k in range(3):
                val_s[k, rows, :] = row[k]

    sub = iota((8, 256), 0)
    lane = iota((8, 256), 1)

    def spread_layer(x, plane_s):
        for h in range(2):
            tiles = [[], [], []]
            for n in range(16):
                pos = pos_ref[n // 8, h, x, 8 * (n % 8) : 8 * (n % 8) + 8, :]
                spot = pos & 127
                for k in range(3):
                    picked = take(val_s[k, 8 * n : 8 * n + 8, :], spot, 1)
                    tiles[k].append(jnp.where(pos >= 0, picked, 0.0))
            for k in range(3):
                plane_s[k, :, 128 * h : 128 * h + 128] = jnp.concatenate(tiles[k], 0).T

    def update_layer(x, plane_s):
        px = jnp.maximum(x - 1, 0)
        first = x == 0
        for yb in range(16):
            rows = slice(8 * yb, 8 * yb + 8)
            m = [h_ref[k, x, rows, :] for k in range(3)]
            behind = [jnp.where(first, below_ref[k, rows, :], h_ref[k + 1, px, rows, :]) for k in range(2)]

            def diff_y(k):
                rolled = pltpu.roll(m[k], 1, 0)
                edge = h_ref[k, x, 8 * yb - 1 : 8 * yb, :] if yb > 0 else jnp.zeros((1, 256), F)
                return m[k] - jnp.where(sub == 0, edge, rolled)

            def diff_z(k):
                return m[k] - jnp.where(lane == 0, 0.0, pltpu.roll(m[k], 1, 1))

            curl = (
                diff_y(2) - diff_z(1),
                diff_z(0) - (m[2] - behind[1]),
                (m[1] - behind[0]) - diff_y(0),
            )
            sigma = sigma_ref[x, rows, :]
            inverse = 1.0 / (1.0 + sigma)
            keep = (1.0 - sigma) * inverse
            push = COURANT * inverse
            for k in range(3):
                eo_ref[k, x, rows, :] = keep * e_ref[k, x, rows, :] + push * (curl[k] - plane_s[k, rows, :])
        pltpu.make_async_copy(eo_ref.at[:, x], eo_hbm.at[:, x], sems.at[x]).start()

    def arrive(x, which):
        for copy in fetch(x)[which]:
            copy.wait()

    early, late = slice(0, 2), slice(2, 5)
    arrive(0, early)
    spread_layer(0, plane_s)

    def two_layers(n, carry):
        x = 2 * n
        arrive(x + 1, early)
        arrive(x, late)
        spread_layer(x + 1, plane_t)
        update_layer(x, plane_s)

        @pl.when(n < 3)
        def _():
            arrive(x + 2, early)

        arrive(x + 1, late)
        spread_layer(jnp.minimum(x + 2, 7), plane_s)
        update_layer(x + 1, plane_t)
        return carry

    lax.fori_loop(0, 4, two_layers, 0)
    for x in range(8):
        pltpu.make_async_copy(eo_ref.at[:, x], eo_hbm.at[:, x], sems.at[x]).wait()


def electrics(electric, magnetic_new, below, conductivity, induced, tangent, found):
    whole = pltpu.VMEM((3, 8, 128, 256), F)
    outside = pl.BlockSpec(memory_space=pltpu.HBM)
    inside = pl.BlockSpec(memory_space=pltpu.VMEM)
    return call(
        electric_kernel,
        shape(3, 8, 128, 256),
        electric, magnetic_new, below, conductivity, induced, tangent, *found,
        name="electrics",
        in_specs=[outside, outside, inside, outside, inside, inside, inside, inside, outside, outside],
        out_specs=outside,
        scratch=[
            pltpu.VMEM((3, 128, 128), F),
            pltpu.VMEM((3, 128, 256), F),
            pltpu.VMEM((3, 128, 256), F),
            whole, whole, whole,
            pltpu.VMEM((8, 128, 256), F),
            pltpu.VMEM((2,) + HALF, I32),
            pltpu.SemaphoreType.DMA((8,)),
            pltpu.SemaphoreType.DMA((5, 8)),
        ],
        limit=53,
        micros=6,
    )


BOTH = ("slab", "cable")


def along(x, axis, by):
    peers = lax.axis_size(axis)
    return lax.ppermute(x, axis, [(i, i + by) for i in range(peers) if 0 <= i + by < peers])


def around(x, axis):
    peers = lax.axis_size(axis)
    return lax.ppermute(x, axis, [(i, (i + 1) % peers) for i in range(peers)])


def exchange(x):
    return lax.all_to_all(x, BOTH, split_axis=0, concat_axis=0, tiled=True)


def local(
    electric, magnetic, conductivity, voltage, current, inverse_inductance,
    inverse_capacitance, tangent, sample_cell, tube_length, junction_link,
):
    cells = sample_cell.reshape(128, 128)
    steer = tangent.reshape(3, 128, 128)
    drive_local, layer = samples(electric, cells, steer)
    above = along(layer, BOTH, -1)
    drive_local, cells = lax.optimization_barrier((drive_local, cells))
    drive = exchange(drive_local)
    cell, perm, pos_a = first_search(cells)
    magnetic_new, layer = magnetics(electric, magnetic, above)
    drive, layer, cell, pos_a = lax.optimization_barrier((drive, layer, cell, pos_a))
    below = along(layer, BOTH, 1)
    *state, ends, induced = lines(
        voltage, current, inverse_inductance, inverse_capacitance, drive, tube_length.reshape(1, 128)
    )
    ends, cell = lax.optimization_barrier((ends, cell))
    ends = around(ends, "cable")
    pos_b = second_search(cell)
    fix, induced = junctions(
        ends, junction_link.reshape(1, 128), inverse_inductance, inverse_capacitance, induced
    )
    induced, pos_b = lax.optimization_barrier((induced, pos_b))
    induced_local = exchange(induced)
    volts, amps = last_voltages(*state, fix)
    electric_new = electrics(electric, magnetic_new, below, conductivity, induced_local, steer, (cell, perm, pos_a, pos_b))
    return electric_new, magnetic_new, volts, amps


def solution(mesh):
    grid = P(None, BOTH, None, None)
    tubes = P(None, None, BOTH)
    return jax.shard_map(
        local,
        mesh=mesh,
        in_specs=(
            grid, grid, P(BOTH, None, None), tubes, tubes, tubes, tubes,
            P(None, BOTH, None), P(BOTH, None), P(BOTH), P(BOTH),
        ),
        out_specs=(grid, grid, tubes, tubes),
        check_vma=False,
    )
```

```python
import jax
import jax.numpy as jnp
from jax import lax
from jax.experimental import pallas as pl
from jax.experimental.pallas import tpu as pltpu
from jax.sharding import PartitionSpec as P

F = jnp.float32
B16 = jnp.bfloat16
I32 = jnp.int32
SUB = 3
COURANT = 0.5
MB = 2**20


def take(x, index, axis):
    return jnp.take_along_axis(x, index, axis=axis, mode="promise_in_bounds")


def iota(shape, axis):
    return lax.broadcasted_iota(I32, shape, axis)


def call(body, out, *ins, name, scratch=(), limit=40, in_specs=None, aliases=None, out_specs=None, micros=None, grid=()):
    kw = {}
    if in_specs is not None:
        kw["in_specs"] = in_specs
    if out_specs is not None:
        kw["out_specs"] = out_specs
    return pl.pallas_call(
        body,
        out_shape=out,
        grid=grid,
        scratch_shapes=list(scratch),
        input_output_aliases=aliases or {},
        compiler_params=pltpu.CompilerParams(vmem_limit_bytes=limit * MB),
        cost_estimate=pl.CostEstimate(flops=0, bytes_accessed=int(micros * 3.69e6), transcendentals=0) if micros else None,
        name=name,
        **kw,
    )(*ins)


def shape(*dims, dtype=F):
    return jax.ShapeDtypeStruct(dims, dtype)


def gather_kernel(e_hbm, idx_hbm, tan_hbm, drive_ref, layer_ref, e_ref, idx_ref, tan_ref, sems):
    copies = [pltpu.make_async_copy(e_hbm.at[:, x], e_ref.at[:, x], sems.at[x]) for x in range(8)]
    idx_copy = pltpu.make_async_copy(idx_hbm, idx_ref, sems.at[8])
    tan_copy = pltpu.make_async_copy(tan_hbm, tan_ref, sems.at[9])
    idx_copy.start()
    for copy in copies:
        copy.start()
    tan_copy.start()
    idx_copy.wait()
    for h in range(2):
        lanes = pl.ds(h * 128, 128)
        rows = pl.ds(h, 64, stride=2)
        idx = idx_ref[rows, :]
        idx = [idx[8 * g : 8 * g + 8] for g in range(8)]
        low = [i & 7 for i in idx]
        high = [i >> 3 for i in idx]
        acc = (jnp.zeros((8, 128), F),) * 24
        for x in range(8):
            if h == 0:
                copies[x].wait()

            def step(yb, acc):
                acc = list(acc)
                yrows = pl.ds(pl.multiple_of(yb * 8, 8), 8)
                src = [e_ref[k, x, yrows, lanes] for k in range(3)]
                for g in range(8):
                    hit = high[g] == yb + 16 * x
                    for k in range(3):
                        acc[g * 3 + k] = jnp.where(hit, take(src[k], low[g], 0), acc[g * 3 + k])
                return tuple(acc)

            acc = lax.fori_loop(0, 16, step, acc, unroll=4)
        if h == 0:
            tan_copy.wait()
            layer_ref[...] = e_ref[1:3, 0]
        picked = [jnp.concatenate([acc[g * 3 + k] for g in range(8)], 0) for k in range(3)]
        steer = [tan_ref[k, rows, :] for k in range(3)]
        drive_ref[rows, :] = steer[0] * picked[0] + steer[1] * picked[1] + steer[2] * picked[2]


def samples(electric, cells, steer):
    return call(
        gather_kernel,
        (shape(128, 128), shape(2, 128, 256)),
        electric, cells, steer,
        name="samples",
        in_specs=[pl.BlockSpec(memory_space=pltpu.HBM)] * 3,
        scratch=[
            pltpu.VMEM((3, 8, 128, 256), F),
            pltpu.VMEM((128, 128), I32),
            pltpu.VMEM((3, 128, 128), F),
            pltpu.SemaphoreType.DMA((10,)),
        ],
        limit=58,
        micros=4,
    )


def merge_pair(x, y):
    low = iota((8, 128), 0) < 4
    return jnp.where(low, x, pltpu.roll(y, 4, 0)), jnp.where(low, pltpu.roll(x, 4, 0), y)


def split_parts(x):
    high = x.astype(B16)
    return high, (x - high.astype(F)).astype(B16)


def product(m_ref, rows, x):
    high, low = split_parts(x)
    rhs = jnp.concatenate([high, low], 1)
    rhs = jnp.concatenate([rhs, rhs], 0)
    y = jnp.dot(m_ref[rows, :], rhs, preferred_element_type=F)
    return y[:, :128] + y[:, 128:]


def line_kernel(
    v_hbm, i_hbm, a_hbm, b_hbm, drive_ref, len_ref,
    vo_hbm, io_hbm, bo_hbm, eg, ends_ref, ind_ref,
    vt, it, at, vg, ig, ah, bh, dg, indt, v_ref, i_ref, a_ref, b_ref, sems, in_sems,
):
    matrices = [
        pltpu.make_async_copy(src, dst, in_sems.at[8 + m])
        for m, (src, dst) in enumerate(((a_hbm, a_ref), (b_hbm, b_ref)))
    ]
    for copy in matrices:
        copy.start()
    arrivals = []
    for q in range(4):
        part = pl.ds(8 * q, 8)
        pair = [
            pltpu.make_async_copy(src.at[part], dst.at[part], in_sems.at[2 * q + m])
            for m, (src, dst) in enumerate(((v_hbm, v_ref), (i_hbm, i_ref)))
        ]
        for copy in pair:
            copy.start()
        arrivals.append(pair)
    sub8 = iota((8, 128), 0)
    lane8 = iota((8, 128), 1)
    lane = iota((128, 128), 1)


    spread = [(sub8 >> 2) + 2 * j for j in range(4)]
    own = (sub8 & 3) == (lane8 & 3)
    for m_ref, dst, arrival in ((a_ref, ah, matrices[0]), (b_ref, bh, matrices[1])):
        arrival.wait()

        def expand(c, carry):
            tiles = []
            for q in range(4):
                tile = m_ref[c, 8 * q : 8 * q + 8, :]
                for j in range(4):
                    tiles.append(jnp.where(own, take(tile, spread[j], 0), 0.0))
            at[c] = jnp.concatenate(tiles, 0).T
            return carry

        lax.fori_loop(0, 32, expand, 0, unroll=4)

        def pack(b, carry):
            rows = pl.ds(pl.multiple_of(b * 8, 8), 8)
            first, second = [], []
            for i in range(16):
                g0, g1 = merge_pair(at[2 * i, rows, :], at[2 * i + 1, rows, :])
                first.append(g0)
                second.append(g1)
            for p, tiles in enumerate((first, second)):
                high, low = split_parts(jnp.concatenate(tiles, 0))
                out_rows = pl.ds(pl.multiple_of(b * 256 + p * 128, 128), 128)
                dst[out_rows, 0:128] = high
                dst[out_rows, 128:256] = low
            return carry

        lax.fori_loop(0, 16, pack, 0, unroll=2)

    results = [pltpu.make_async_copy(bh, bo_hbm, sems.at[0])]
    results[0].start()

    def turn_in(c, carry):
        vt[c] = v_ref[c].T
        it[c] = i_ref[c].T
        return carry

    for q in range(4):
        for copy in arrivals[q]:
            copy.wait()
        lax.fori_loop(8 * q, 8 * q + 8, turn_in, 0, unroll=4)
    def regroup(b, carry):
        rows = pl.ds(pl.multiple_of(b * 8, 8), 8)
        for src, dst in ((vt, vg), (it, ig)):
            for i in range(16):
                g0, g1 = merge_pair(src[2 * i, rows, :], src[2 * i + 1, rows, :])
                dst[pl.ds(pl.multiple_of(b * 256 + 8 * i, 8), 8), :] = g0
                dst[pl.ds(pl.multiple_of(b * 256 + 128 + 8 * i, 8), 8), :] = g1
        return carry

    lax.fori_loop(0, 16, regroup, 0, unroll=2)

    at[0] = drive_ref[...].T
    at[1] = jnp.broadcast_to(len_ref[...].astype(F), (128, 128)).T
    for b in range(16):
        rows = slice(8 * b, 8 * b + 8)
        for p, value in enumerate(merge_pair(at[0, rows, :], at[0, rows, :])):
            dg[16 * b + 8 * p : 16 * b + 8 * p + 8, :] = value
        for p, value in enumerate(merge_pair(at[1, rows, :], at[1, rows, :])):
            eg[16 * b + 8 * p : 16 * b + 8 * p + 8, :] = value.astype(I32)

    unroll = 16
    for substep in range(SUB):

        def current_step(n, acc):
            for u in range(unroll):
                g = n * unroll + u
                rows = pl.ds(pl.multiple_of(g * 128, 128), 128)
                small = pl.ds(pl.multiple_of(g * 8, 8), 8)
                length = eg[small, :]
                live = jnp.concatenate([lane8 < length] * 16, 0)
                drive = jnp.concatenate([dg[small, :]] * 16, 0)
                volts = vg[rows, :]
                ahead = jnp.where(lane == 127, 0.0, pltpu.roll(volts, 127, 1))
                y = product(ah, rows, ahead - volts - drive)
                amps = jnp.where(live, ig[rows, :] - y, 0.0)
                ig[rows, :] = amps
                spot = lane8 == 4 * g + (sub8 & 3)
                acc = tuple(
                    jnp.where(spot, take(amps[8 * i : 8 * i + 8], length - 1, 1), acc[i])
                    for i in range(16)
                )
            return acc

        acc = lax.fori_loop(0, 32 // unroll, current_step, (jnp.zeros((8, 128), F),) * 16)
        pick = (sub8 & 1) * 4 + (lane8 & 3)
        for q in range(4):
            out = take(acc[4 * q], pick, 0)
            for i in range(1, 4):
                out = jnp.where((sub8 >> 1) == i, take(acc[4 * q + i], pick, 0), out)
            ends_ref[substep, 8 * q : 8 * q + 8, :] = out

        if substep == SUB - 1:
            break

        def voltage_step(n, carry):
            for u in range(unroll):
                g = n * unroll + u
                rows = pl.ds(pl.multiple_of(g * 128, 128), 128)
                small = pl.ds(pl.multiple_of(g * 8, 8), 8)
                live = jnp.concatenate([lane8 < eg[small, :]] * 16, 0)
                amps = ig[rows, :]
                behind = jnp.where(lane == 0, 0.0, pltpu.roll(amps, 1, 1))
                y = product(bh, rows, amps - behind)
                vg[rows, :] = jnp.where(live, vg[rows, :] - y, 0.0)
            return carry

        lax.fori_loop(0, 32 // unroll, voltage_step, 0)
        if substep == SUB - 2:
            results.append(pltpu.make_async_copy(vg, vo_hbm, sems.at[1]))
            results[1].start()

    results.append(pltpu.make_async_copy(ig, io_hbm, sems.at[2]))
    results[2].start()

    def average(b, carry):
        totals = []
        for p in range(2):
            tiles = [ig[pl.ds(pl.multiple_of(b * 256 + 128 * p + 8 * i, 8), 8), :] for i in range(16)]
            while len(tiles) > 1:
                tiles = [x + y for x, y in zip(tiles[::2], tiles[1::2])]
            totals.append(tiles[0] + pltpu.roll(tiles[0], 4, 0))
        indt[pl.ds(pl.multiple_of(b * 8, 8), 8), :] = jnp.where(sub8 < 4, totals[0], totals[1]) * (1.0 / 32.0)
        return carry

    lax.fori_loop(0, 16, average, 0, unroll=4)
    ind_ref[...] = indt[...].T
    for copy in results:
        copy.wait()


def last_kernel(
    v_hbm, i_hbm, b_hbm, eg, fix_ref,
    vo_hbm, io_hbm,
    vt, it, vg, ig, bh, vo_ref, io_ref, sems, in_sems,
):
    sub8 = iota((8, 128), 0)
    lane8 = iota((8, 128), 1)
    lane = iota((128, 128), 1)
    arrivals = []
    for q in range(4):
        part = pl.ds(1024 * q, 1024)
        group = [
            pltpu.make_async_copy(src.at[part], dst.at[part], in_sems.at[m, q])
            for m, (src, dst) in enumerate(((i_hbm, ig), (b_hbm, bh), (v_hbm, vg)))
        ]
        for copy in group:
            copy.start()
        arrivals.append(group)

    for q in range(4):
        for copy in arrivals[q]:
            copy.wait()
        for u in range(8):
            g = q * 8 + u
            rows = slice(g * 128, g * 128 + 128)
            live = jnp.concatenate([lane8 < eg[8 * g : 8 * g + 8, :]] * 16, 0)
            amps = ig[rows, :]
            behind = jnp.where(lane == 0, 0.0, pltpu.roll(amps, 1, 1))
            y = product(bh, rows, amps - behind)
            vg[rows, :] = jnp.where(live, vg[rows, :] - y, 0.0)

    def ungroup(b, carry):
        rows = pl.ds(pl.multiple_of(b * 8, 8), 8)
        for src, dst in ((vg, vt), (ig, it)):
            for i in range(16):
                g0 = src[pl.ds(pl.multiple_of(b * 256 + 8 * i, 8), 8), :]
                g1 = src[pl.ds(pl.multiple_of(b * 256 + 128 + 8 * i, 8), 8), :]
                dst[2 * i, rows, :], dst[2 * i + 1, rows, :] = merge_pair(g0, g1)
        return carry

    lax.fori_loop(0, 16, ungroup, 0, unroll=2)
    copies = []
    for q in range(4):

        def turn_out(n, carry):
            c = 8 * q + n
            row = pl.ds(c, 1)
            v = vt[c].T
            i = it[c].T
            first = sub8 == 0
            second = sub8 == 1
            fix = [fix_ref[m, row, :] for m in range(5)]
            vo_ref[c] = v
            io_ref[c] = i
            vo_ref[c, 0:8, :] = v[0:8] + jnp.where(
                first, fix[0], jnp.where(second, fix[1], jnp.where(sub8 == 2, fix[2], 0.0))
            )
            io_ref[c, 0:8, :] = i[0:8] + jnp.where(first, fix[3], jnp.where(second, fix[4], 0.0))
            return carry

        lax.fori_loop(0, 8, turn_out, 0, unroll=4)
        part = pl.ds(8 * q, 8)
        for m, (src, dst) in enumerate(((vo_ref, vo_hbm), (io_ref, io_hbm))):
            copy = pltpu.make_async_copy(src.at[part], dst.at[part], sems.at[m, q])
            copy.start()
            copies.append(copy)
    for copy in copies:
        copy.wait()


def lines(voltage, current, inductance, capacitance, drive, lengths):
    big = pltpu.VMEM((32, 128, 128), F)
    flat = pltpu.VMEM((4096, 128), F)
    packed = pltpu.VMEM((4096, 256), B16)
    outside = pl.BlockSpec(memory_space=pltpu.HBM)
    inside = pl.BlockSpec(memory_space=pltpu.VMEM)
    return call(
        line_kernel,
        (shape(4096, 128), shape(4096, 128), shape(4096, 256, dtype=B16), shape(256, 128, dtype=I32),
         shape(3, 32, 128), shape(128, 128)),
        voltage, current, inductance, capacitance, drive, lengths,
        name="lines",
        in_specs=[outside] * 4 + [inside] * 2,
        out_specs=(outside, outside, outside, inside, inside, inside),
        scratch=[big, big, big, flat, flat, packed, packed, pltpu.VMEM((256, 128), F),
                 pltpu.VMEM((128, 128), F), big, big,
                 pltpu.VMEM((32, 32, 128), F), pltpu.VMEM((32, 32, 128), F),
                 pltpu.SemaphoreType.DMA((3,)), pltpu.SemaphoreType.DMA((10,))],
        limit=53,
        micros=16,
    )


def last_voltages(volts, amps, capacitance, ends_at, fix):
    big = pltpu.VMEM((32, 128, 128), F)
    flat = pltpu.VMEM((4096, 128), F)
    outside = pl.BlockSpec(memory_space=pltpu.HBM)
    inside = pl.BlockSpec(memory_space=pltpu.VMEM)
    return call(
        last_kernel,
        (shape(32, 128, 128), shape(32, 128, 128)),
        volts, amps, capacitance, ends_at, fix,
        name="last_voltages",
        in_specs=[outside] * 3 + [inside] * 2,
        out_specs=(outside, outside),
        scratch=[big, big, flat, flat, pltpu.VMEM((4096, 256), B16), big, big,
                 pltpu.SemaphoreType.DMA((2, 4)), pltpu.SemaphoreType.DMA((3, 4))],
        limit=53,
        micros=6,
    )


def junction_kernel(ends_ref, link_ref, a_ref, b_ref, ind_ref, fix_ref, indo_ref, buf):
    link = jnp.broadcast_to(link_ref[...], (8, 128))
    inflow = [
        jnp.concatenate([take(ends_ref[k, 8 * q : 8 * q + 8, :], link, 1) for q in range(4)], 0)
        for k in range(SUB)
    ]

    def apply(m_ref, x):
        buf[...] = x
        parts = [None] * 4
        for d in range(32):
            term = m_ref[d] * buf[d : d + 1, :]
            parts[d % 4] = term if parts[d % 4] is None else parts[d % 4] + term
        return (parts[0] + parts[1]) + (parts[2] + parts[3])

    f1, f2, f3 = inflow
    v1 = apply(b_ref, f1)
    i2 = apply(a_ref, v1)
    v2b = apply(b_ref, i2)
    v2a = v1 - v2b + apply(b_ref, f2)
    i3a = i2 - apply(a_ref, v2b - v2a)
    i3b = apply(a_ref, v2b)
    v3c = apply(b_ref, i3b)
    v3a = v2a - apply(b_ref, i3a - f3)
    v3b = v2b - v3c + apply(b_ref, i3a)
    sub8 = iota((8, 128), 0)
    for n, value in enumerate((v3a, v3b, v3c, i3a, i3b)):
        fix_ref[n] = value
    mean_a = jnp.sum(i3a, axis=0, keepdims=True) * (1.0 / 32.0)
    mean_b = jnp.sum(i3b, axis=0, keepdims=True) * (1.0 / 32.0)
    indo_ref[...] = ind_ref[...]
    indo_ref[0:8, :] = ind_ref[0:8, :] + jnp.where(sub8 == 0, mean_a, jnp.where(sub8 == 1, mean_b, 0.0))


def junctions(ends, link, inductance, capacitance, induced):
    return call(
        junction_kernel,
        (shape(5, 32, 128), shape(128, 128)),
        ends, link, inductance, capacitance, induced,
        name="junctions",
        scratch=[pltpu.VMEM((32, 128), F)],
        limit=3,
        micros=1,
    )


def magnetic_kernel(e_hbm, h_hbm, above_ref, ho_hbm, layer_ref, e_ref, h_ref, ho_ref, sems):
    sub = iota((8, 256), 0)
    lane = iota((8, 256), 1)

    def fetch(x):
        return (
            pltpu.make_async_copy(e_hbm.at[:, x], e_ref.at[:, x], sems.at[0, x]),
            pltpu.make_async_copy(h_hbm.at[:, x], h_ref.at[:, x], sems.at[1, x]),
        )

    def store(x):
        return pltpu.make_async_copy(ho_ref.at[:, x], ho_hbm.at[:, x], sems.at[2, x])

    for x in range(8):
        for copy in fetch(x):
            copy.start()
    fetch(0)[0].wait()

    def one_layer(x, carry):
        nx = jnp.minimum(x + 1, 7)
        last = x == 7
        for yb in range(16):
            rows = slice(8 * yb, 8 * yb + 8)
            e = [e_ref[k, x, rows, :] for k in range(3)]
            ahead = [jnp.where(last, above_ref[k, rows, :], e_ref[k + 1, nx, rows, :]) for k in range(2)]

            def diff_y(k):
                rolled = pltpu.roll(e[k], 7, 0)
                edge = e_ref[k, x, 8 * yb + 8 : 8 * yb + 9, :] if yb < 15 else jnp.zeros((1, 256), F)
                return jnp.where(sub == 7, edge, rolled) - e[k]

            def diff_z(k):
                return jnp.where(lane == 255, 0.0, pltpu.roll(e[k], 255, 1)) - e[k]

            curl = (
                diff_y(2) - diff_z(1),
                diff_z(0) - (ahead[1] - e[2]),
                (ahead[0] - e[1]) - diff_y(0),
            )
            for k in range(3):
                ho_ref[k, x, rows, :] = h_ref[k, x, rows, :] - COURANT * curl[k]
        return carry

    def layer_step(x, carry):
        @pl.when(x < 7)
        def _():
            fetch(x + 1)[0].wait()

        fetch(x)[1].wait()
        one_layer(x, carry)
        store(x).start()
        return carry

    lax.fori_loop(0, 8, layer_step, 0)
    layer_ref[...] = ho_ref[1:3, 7]
    for x in range(8):
        store(x).wait()


def magnetics(electric, magnetic, above):
    whole = pltpu.VMEM((3, 8, 128, 256), F)
    outside = pl.BlockSpec(memory_space=pltpu.HBM)
    inside = pl.BlockSpec(memory_space=pltpu.VMEM)
    return call(
        magnetic_kernel,
        (shape(3, 8, 128, 256), shape(2, 128, 256)),
        electric, magnetic, above,
        name="magnetics",
        in_specs=[outside, outside, inside],
        out_specs=(outside, inside),
        scratch=[whole, whole, whole, pltpu.SemaphoreType.DMA((3, 8))],
        limit=53,
        micros=4,
    )


def sort_columns(keys):
    sub8 = iota((8, 128), 0)
    keys = list(keys)
    size = 2
    while size <= 128:
        stride = size // 2
        while stride >= 1:
            if stride >= 8:
                gap = stride // 8
                for n in range(16):
                    if n & gap:
                        continue
                    rising = ((n * 8) & size) == 0 or size == 128
                    low = jnp.minimum(keys[n], keys[n + gap])
                    high = jnp.maximum(keys[n], keys[n + gap])
                    keys[n], keys[n + gap] = (low, high) if rising else (high, low)
            else:
                partner = sub8 ^ stride
                first = (sub8 & stride) == 0
                for n in range(16):
                    other = take(keys[n], partner, 0)
                    if size >= 8:
                        rising = ((n * 8) & size) == 0 or size == 128
                        want_low = first if rising else ~first
                    else:
                        want_low = ((sub8 & size) == 0) == first
                    keys[n] = jnp.where(want_low, jnp.minimum(keys[n], other), jnp.maximum(keys[n], other))
            stride //= 2
        size *= 2
    return keys


def sort_cells(idx_ref, cell_ref, perm_ref):
    sub8 = iota((8, 128), 0)
    keys = []
    for n in range(16):
        owner = sub8 + 8 * n
        cell = idx_ref[8 * n : 8 * n + 8, :]
        keys.append(((owner & 1) * 1024 + cell) * 128 + owner)
    keys = jnp.concatenate(sort_columns(keys), 0).T
    cell_ref[...] = keys >> 7
    perm_ref[...] = keys & 127


def find_cells(cell_ref, pos_hbm, start, pos_ref, sems):
    lane8 = iota((8, 128), 1)

    def spread(n, carry):
        rows = pl.ds(pl.multiple_of(n * 8, 8), 8)
        cell = cell_ref[pl.ds(pl.multiple_of(start + n * 8, 8), 8), :]
        for h in range(2):
            fence = {
                p: take(cell, jnp.full((8, 128), 64 * h + p, I32), 1)
                for p in (0, 8, 16, 24, 32, 40, 48, 56)
            }
            chains = []
            for x in range(8):
                target = lane8 + (h * 1024 + x * 128)
                up = fence[32] <= target
                pos = jnp.where(up, 64 * h + 32, 64 * h)
                cur = jnp.where(up, fence[32], fence[0])
                probe = jnp.where(up, fence[48], fence[16])
                up2 = probe <= target
                pos = jnp.where(up2, pos + 16, pos)
                cur = jnp.where(up2, probe, cur)
                probe = jnp.where(
                    up,
                    jnp.where(up2, fence[56], fence[40]),
                    jnp.where(up2, fence[24], fence[8]),
                )
                hit = probe <= target
                chains.append((target, jnp.where(hit, pos + 8, pos), jnp.where(hit, probe, cur)))
            for step in (4, 2, 1):
                probes = [take(cell, pos + step, 1) for _, pos, _ in chains]
                hits = [probe <= chain[0] for probe, chain in zip(probes, chains)]
                chains = [
                    (target, jnp.where(hit, pos + step, pos), jnp.where(hit, probe, cur))
                    for (target, pos, cur), probe, hit in zip(chains, probes, hits)
                ]
            for x, (target, pos, cur) in enumerate(chains):
                pos_ref[h, x, rows, :] = jnp.where(cur == target, pos, -1)
        return carry

    copies = []
    for part in range(4):
        lax.fori_loop(2 * part, 2 * part + 2, spread, 0)
        rows = pl.ds(16 * part, 16)
        copies.append(pltpu.make_async_copy(pos_ref.at[:, :, rows], pos_hbm.at[:, :, rows], sems.at[part]))
        copies[part].start()
    for copy in copies:
        copy.wait()


def first_search_kernel(idx_ref, cell_ref, perm_ref, pos_hbm, pos_ref, sems):
    sort_cells(idx_ref, cell_ref, perm_ref)
    find_cells(cell_ref, pos_hbm, 0, pos_ref, sems)


def second_search_kernel(cell_ref, pos_hbm, pos_ref, sems):
    find_cells(cell_ref, pos_hbm, 64, pos_ref, sems)


HALF = (2, 8, 64, 128)


def first_search(cells):
    inside = pl.BlockSpec(memory_space=pltpu.VMEM)
    return call(
        first_search_kernel,
        (shape(128, 128, dtype=I32), shape(128, 128, dtype=I32), pltpu.HBM(HALF, I32)),
        cells,
        name="first_search",
        out_specs=(inside, inside, pl.BlockSpec(memory_space=pltpu.HBM)),
        scratch=[pltpu.VMEM(HALF, I32), pltpu.SemaphoreType.DMA((4,))],
        limit=53,
        micros=3,
    )


def second_search(cell):
    return call(
        second_search_kernel,
        pltpu.HBM(HALF, I32),
        cell,
        name="second_search",
        out_specs=pl.BlockSpec(memory_space=pltpu.HBM),
        scratch=[pltpu.VMEM(HALF, I32), pltpu.SemaphoreType.DMA((4,))],
        limit=53,
        micros=3,
    )


def search(cells):
    cell, perm, pos = first_search(cells)
    return cell, perm, pos, second_search(cell)


def electric_kernel(
    e_hbm, h_hbm, below_ref, sigma_hbm, ind_ref, tan_ref, cell_s, perm_s, pos_a, pos_b,
    eo_hbm, val_s, plane_s, plane_t, eo_ref, e_ref, h_ref, sigma_ref, pos_ref, sems, in_sems,
):
    def fetch(x):
        return (
            pltpu.make_async_copy(pos_a.at[:, x], pos_ref.at[0, :, x], in_sems.at[0, x]),
            pltpu.make_async_copy(pos_b.at[:, x], pos_ref.at[1, :, x], in_sems.at[4, x]),
            pltpu.make_async_copy(h_hbm.at[:, x], h_ref.at[:, x], in_sems.at[1, x]),
            pltpu.make_async_copy(e_hbm.at[:, x], e_ref.at[:, x], in_sems.at[2, x]),
            pltpu.make_async_copy(sigma_hbm.at[x], sigma_ref.at[x], in_sems.at[3, x]),
        )

    for x in range(8):
        for copy in fetch(x):
            copy.start()
    for k in range(3):
        val_s[k] = (tan_ref[k] * ind_ref[...]).T
    for start in range(0, 16, 8):
        spans = [slice(8 * n, 8 * n + 8) for n in range(start, start + 8)]
        cells = [cell_s[rows, :] for rows in spans]
        val = [[take(val_s[k, rows, :], perm_s[rows, :], 1) for k in range(3)] for rows in spans]
        for gap in (1, 2, 4, 8, 16, 32):
            same = [pltpu.roll(cell, gap, 1) == cell for cell in cells]
            moved = [[pltpu.roll(v, gap, 1) for v in row] for row in val]
            val = [
                [v + jnp.where(hit, w, 0.0) for v, w in zip(row, shifted)]
                for row, shifted, hit in zip(val, moved, same)
            ]
        for rows, row in zip(spans, val):
            for k in range(3):
                val_s[k, rows, :] = row[k]

    sub = iota((8, 256), 0)
    lane = iota((8, 256), 1)

    def spread_layer(x, plane_s):
        for h in range(2):
            tiles = [[], [], []]
            for n in range(16):
                pos = pos_ref[n // 8, h, x, 8 * (n % 8) : 8 * (n % 8) + 8, :]
                spot = pos & 127
                for k in range(3):
                    picked = take(val_s[k, 8 * n : 8 * n + 8, :], spot, 1)
                    tiles[k].append(jnp.where(pos >= 0, picked, 0.0))
            for k in range(3):
                plane_s[k, :, 128 * h : 128 * h + 128] = jnp.concatenate(tiles[k], 0).T

    def update_layer(x, plane_s):
        px = jnp.maximum(x - 1, 0)
        first = x == 0
        for yb in range(16):
            rows = slice(8 * yb, 8 * yb + 8)
            m = [h_ref[k, x, rows, :] for k in range(3)]
            behind = [jnp.where(first, below_ref[k, rows, :], h_ref[k + 1, px, rows, :]) for k in range(2)]

            def diff_y(k):
                rolled = pltpu.roll(m[k], 1, 0)
                edge = h_ref[k, x, 8 * yb - 1 : 8 * yb, :] if yb > 0 else jnp.zeros((1, 256), F)
                return m[k] - jnp.where(sub == 0, edge, rolled)

            def diff_z(k):
                return m[k] - jnp.where(lane == 0, 0.0, pltpu.roll(m[k], 1, 1))

            curl = (
                diff_y(2) - diff_z(1),
                diff_z(0) - (m[2] - behind[1]),
                (m[1] - behind[0]) - diff_y(0),
            )
            sigma = sigma_ref[x, rows, :]
            inverse = 1.0 / (1.0 + sigma)
            keep = (1.0 - sigma) * inverse
            push = COURANT * inverse
            for k in range(3):
                eo_ref[k, x, rows, :] = keep * e_ref[k, x, rows, :] + push * (curl[k] - plane_s[k, rows, :])
        pltpu.make_async_copy(eo_ref.at[:, x], eo_hbm.at[:, x], sems.at[x]).start()

    def arrive(x, which):
        for copy in fetch(x)[which]:
            copy.wait()

    early, late = slice(0, 2), slice(2, 5)
    arrive(0, early)
    spread_layer(0, plane_s)

    def two_layers(n, carry):
        x = 2 * n
        arrive(x + 1, early)
        arrive(x, late)
        spread_layer(x + 1, plane_t)
        update_layer(x, plane_s)

        @pl.when(n < 3)
        def _():
            arrive(x + 2, early)

        arrive(x + 1, late)
        spread_layer(jnp.minimum(x + 2, 7), plane_s)
        update_layer(x + 1, plane_t)
        return carry

    lax.fori_loop(0, 4, two_layers, 0)
    for x in range(8):
        pltpu.make_async_copy(eo_ref.at[:, x], eo_hbm.at[:, x], sems.at[x]).wait()


def electrics(electric, magnetic_new, below, conductivity, induced, tangent, found):
    whole = pltpu.VMEM((3, 8, 128, 256), F)
    outside = pl.BlockSpec(memory_space=pltpu.HBM)
    inside = pl.BlockSpec(memory_space=pltpu.VMEM)
    return call(
        electric_kernel,
        shape(3, 8, 128, 256),
        electric, magnetic_new, below, conductivity, induced, tangent, *found,
        name="electrics",
        in_specs=[outside, outside, inside, outside, inside, inside, inside, inside, outside, outside],
        out_specs=outside,
        scratch=[
            pltpu.VMEM((3, 128, 128), F),
            pltpu.VMEM((3, 128, 256), F),
            pltpu.VMEM((3, 128, 256), F),
            whole, whole, whole,
            pltpu.VMEM((8, 128, 256), F),
            pltpu.VMEM((2,) + HALF, I32),
            pltpu.SemaphoreType.DMA((8,)),
            pltpu.SemaphoreType.DMA((5, 8)),
        ],
        limit=53,
        micros=6,
    )


BOTH = ("slab", "cable")


def along(x, axis, by):
    peers = lax.axis_size(axis)
    return lax.ppermute(x, axis, [(i, i + by) for i in range(peers) if 0 <= i + by < peers])


def around(x, axis):
    peers = lax.axis_size(axis)
    return lax.ppermute(x, axis, [(i, (i + 1) % peers) for i in range(peers)])


def exchange(x):
    return lax.all_to_all(x, BOTH, split_axis=0, concat_axis=0, tiled=True)


def local(
    electric, magnetic, conductivity, voltage, current, inverse_inductance,
    inverse_capacitance, tangent, sample_cell, tube_length, junction_link,
):
    cells = sample_cell.reshape(128, 128)
    steer = tangent.reshape(3, 128, 128)
    drive_local, layer = samples(electric, cells, steer)
    above = along(layer, BOTH, -1)
    drive_local, cells = lax.optimization_barrier((drive_local, cells))
    drive = exchange(drive_local)
    cell, perm, pos_a = first_search(cells)
    magnetic_new, layer = magnetics(electric, magnetic, above)
    drive, layer, cell, pos_a = lax.optimization_barrier((drive, layer, cell, pos_a))
    below = along(layer, BOTH, 1)
    *state, ends, induced = lines(
        voltage, current, inverse_inductance, inverse_capacitance, drive, tube_length.reshape(1, 128)
    )
    ends, cell = lax.optimization_barrier((ends, cell))
    ends = around(ends, "cable")
    pos_b = second_search(cell)
    fix, induced = junctions(
        ends, junction_link.reshape(1, 128), inverse_inductance, inverse_capacitance, induced
    )
    induced, pos_b = lax.optimization_barrier((induced, pos_b))
    induced_local = exchange(induced)
    volts, amps = last_voltages(*state, fix)
    electric_new = electrics(electric, magnetic_new, below, conductivity, induced_local, steer, (cell, perm, pos_a, pos_b))
    return electric_new, magnetic_new, volts, amps


def solution(mesh):
    grid = P(None, BOTH, None, None)
    tubes = P(None, None, BOTH)
    return jax.shard_map(
        local,
        mesh=mesh,
        in_specs=(
            grid, grid, P(BOTH, None, None), tubes, tubes, tubes, tubes,
            P(None, BOTH, None), P(BOTH, None), P(BOTH), P(BOTH),
        ),
        out_specs=(grid, grid, tubes, tubes),
        check_vma=False,
    )
```
